128 devices in a mesh: lon: 16 (over y, z), lat: 8 (over x, core).
Axes of the slice: x: 4, y: 4, z: 4, core: 2. Of those that a mesh axis runs over, the one named last changes fastest.
Arguments:
- layers: float32 [6, 100, 256, 2048], P(None, None, 'lat', 'lon'), may hold values from -4 to 4, as said below
- kmt: int32 [256, 2048], P('lat', 'lon'), may hold values from 0 to 100, as said below
- barotropic: float32 [3, 256, 2048], P(None, 'lat', 'lon'), may hold values from -3 to 3
Outputs:
- layers_new: float32 [6, 100, 256, 2048], P(None, None, 'lat', 'lon')
- barotropic_new: float32 [3, 256, 2048], P(None, 'lat', 'lon')
The draws below stay inside these ranges and needn't reach their ends.
Inputs may be any that keep to these rules, and one draw needn't show every extreme that they name: kmt is 0 on the first and the last row of the grid, on whole land blocks of 8 x 16 columns and on scattered coastal columns; elsewhere it is 1 to 100. `layers`: component 2 (thickness) lies between 0.5 and 2.
All inputs are finite; a program needn't handle non-finite values.
Results may differ from the reference program's by a relative error of at most 0.00002.
Values sent between devices are 32-bit elements; how exact they have to be, the bound alone decides.
A program may use at most 256 MiB of HBM per device.

```python
import math
import jax
import jax.numpy as jnp
from jax import lax

K = 100
NSUB = 16
NY = 256
NX = 2048


def draw_layers(key, part):
    key = jax.random.fold_in(key, 37)
    keys = jax.random.split(key, 3)
    velocity = 0.5 * jnp.clip(jax.random.normal(keys[0], (2, K, NY, NX), jnp.float32), -4.0, 4.0)
    tracer = jnp.clip(jax.random.normal(keys[2], (3, K, NY, NX), jnp.float32), -4.0, 4.0)
    thick = jnp.exp(jax.random.uniform(keys[1], (1, K, NY, NX), jnp.float32, math.log(0.5), math.log(2.0)))
    return jnp.concatenate([velocity, thick, tracer], axis=0).astype(jnp.float32)


def draw_kmt(key, part):
    key = jax.random.fold_in(key, 23)
    keys = jax.random.split(key, 3)
    tiles = jax.random.randint(keys[0], (NY // 8, NX // 16), 0, 4)
    land = jnp.repeat(jnp.repeat(tiles == 0, 8, axis=0), 16, axis=1)
    coast = jax.random.randint(keys[1], (NY, NX), 0, 8) == 0
    depth = jax.random.randint(keys[2], (NY, NX), 1, K + 1)
    rows_index = jnp.arange(NY, dtype=jnp.int32)[:, None]
    walls = (rows_index == 0) | (rows_index == NY - 1)
    return jnp.where(land | coast | walls, 0, depth).astype(jnp.int32)


def shard_levels(own_key, extent, cuts, least, largest):
    factor_of, own = 1.0, jax.random.fold_in(own_key, 6)
    for axis_at, blocks in cuts:
        steps = jnp.exp(jax.random.uniform(jax.random.fold_in(own, axis_at), (blocks,), jnp.float32, least / len(cuts), largest / len(cuts)))
        factor_of = factor_of * jnp.repeat(steps, extent[axis_at] // blocks).reshape([-1 if axis == axis_at else 1 for axis in range(len(extent))])
    return factor_of


def gaussian(own_key, dims, deviation, reach, cuts=(), kind=jnp.bfloat16):
    factor_of = shard_levels(own_key, dims, cuts, -0.22, 0.18) if cuts else 1.0
    drawn = jax.random.normal(own_key, dims, jnp.float32) * deviation * factor_of
    return jnp.minimum(jnp.maximum(drawn, -reach), reach).astype(kind)


def setup_inputs(seed: int = 0) -> dict:
    key_list = jax.random.split(jax.random.key(seed), 4)
    layers = draw_layers(jax.random.fold_in(key_list[3], 71), 0)
    kmt = draw_kmt(jax.random.fold_in(key_list[3], 71), 0)
    barotropic = gaussian(key_list[2], (3, NY, NX), 0.5, 3.0, ((1, 8), (2, 16)), jnp.float32)
    return dict(layers=layers, kmt=kmt, barotropic=barotropic)


time_step = 0.1
sub_step = 0.6
hyper_visc = 0.01
diffusivity = 0.1
gravity = 0.1
thermal = 1.0
haline = 0.8
rotation = 0.5


def pad_grid(field, width):
    config = [(0, 0)] * (field.ndim - 2) + [(width, width), (0, 0)]
    padded = jnp.pad(field, config)
    return jnp.concatenate([padded[..., -width:], padded, padded[..., :width]], axis=-1)


def trim_rim(field, width):
    if width == 0:
        return field
    return field[..., width:-width, width:-width]


def east_diff(field):
    return 0.5 * (field[..., 1:-1, 2:] - field[..., 1:-1, :-2])


def north_diff(field):
    return 0.5 * (field[..., 2:, 1:-1] - field[..., :-2, 1:-1])


def laplace(field):
    return field[..., 2:, 1:-1] + field[..., :-2, 1:-1] + field[..., 1:-1, 2:] + field[..., 1:-1, :-2] - 4.0 * field[..., 1:-1, 1:-1]


def pressure(thick, temper, saline):
    weight = gravity * (haline * saline - thermal * temper) * thick
    return jnp.cumsum(weight, axis=0) - 0.5 * weight


def depth_mean(values, thick, column_total):
    return jnp.sum(values * thick, axis=-3) / jnp.maximum(column_total, 1.0)


def baroclinic(vel_wide, scalar_wide, level_mask, coriolis):
    press = pressure(scalar_wide[0], scalar_wide[1], scalar_wide[2])
    velocity = trim_rim(vel_wide, 2)
    thick = trim_rim(scalar_wide[0], 1)
    column_total = jnp.sum(thick, axis=0)
    tend_east = (-east_diff(press) + coriolis * velocity[1] - hyper_visc * laplace(laplace(vel_wide[0]))) * level_mask
    tend_north = (-north_diff(press) - coriolis * velocity[0] - hyper_visc * laplace(laplace(vel_wide[1]))) * level_mask
    tendency = jnp.stack([tend_east, tend_north])
    forcing = depth_mean(tendency, thick, column_total)
    provisional = (velocity + time_step * (tendency - forcing[:, None])) * level_mask
    clinic = (provisional - depth_mean(provisional, thick, column_total)[:, None]) * level_mask
    return clinic, forcing, column_total / K


def transport(thick, tracer, flow_wide, scalar_wide, level_mask):
    thick_wide = scalar_wide[0]
    tracer_wide = scalar_wide[1:4]
    flux_east = thick_wide * flow_wide[0]
    flux_north = thick_wide * flow_wide[1]
    thick_new = (thick - time_step * (east_diff(flux_east) + north_diff(flux_north))) * level_mask
    content = (thick * tracer - time_step * (east_diff(flux_east * tracer_wide) + north_diff(flux_north * tracer_wide)) + time_step * diffusivity * laplace(tracer_wide)) * level_mask
    return thick_new, content


def reference(layers, kmt, barotropic):
    levels = jnp.arange(K, dtype=jnp.int32)[:, None, None]
    level_mask = (levels < kmt[None]).astype(jnp.float32)
    column_mask = (kmt > 0).astype(jnp.float32)
    fields = layers * level_mask
    rows_global = jnp.arange(NY, dtype=jnp.float32)
    coriolis = (rotation * (2.0 * (rows_global + 0.5) / NY - 1.0))[:, None]
    vel_wide = pad_grid(fields[0:2], 2)
    scalar_wide = pad_grid(fields[2:6], 1)
    clinic, forcing, depth_bar = baroclinic(vel_wide, scalar_wide, level_mask, coriolis)
    surface = barotropic * column_mask

    def subcycle(step, carry):
        height, east, north, sum_east, sum_north = carry
        height = (height - sub_step * (east_diff(pad_grid(depth_bar * east, 1)) + north_diff(pad_grid(depth_bar * north, 1)))) * column_mask
        height_wide = pad_grid(height, 1)
        east = (east + sub_step * (forcing[0] - east_diff(height_wide))) * column_mask
        north = (north + sub_step * (forcing[1] - north_diff(height_wide))) * column_mask
        return height, east, north, sum_east + east, sum_north + north

    zeros = jnp.zeros_like(surface[0])
    final = lax.fori_loop(0, NSUB, subcycle, (surface[0], surface[1], surface[2], zeros, zeros))
    mean_flow = jnp.stack([final[3], final[4]]) / NSUB
    vel_new = (clinic + mean_flow[:, None]) * level_mask
    flow_wide = pad_grid(vel_new, 1)
    thick_new, content = transport(fields[2], fields[3:6], flow_wide, scalar_wide, level_mask)
    layers_new = jnp.concatenate([vel_new, thick_new[None], content], axis=0)
    return layers_new, jnp.stack([final[0], final[1], final[2]])
```

```python
import jax
import jax.numpy as jnp
from jax import lax
from jax.experimental import pallas as pl
from jax.experimental.pallas import tpu as pltpu
from jax.sharding import PartitionSpec as P

K = 100
NSUB = 16
R = 32
C = 128
CH = 25
NY = 256

DT = 0.1
TAU = 0.6
NU = 0.01
KAPPA = 0.1
GRAV = 0.1
THERMAL = 1.0
HALINE = 0.8
ROT = 0.5

F32 = jnp.float32
MESH = pl.DeviceIdType.MESH


def lanes(shape=(1, C)):
    return lax.broadcasted_iota(jnp.int32, shape, 1)


def sublanes(shape):
    return lax.broadcasted_iota(jnp.int32, shape, 0)


def roll(x, s):
    if isinstance(s, int):
        s %= C
        if s == 0:
            return x
    return pltpu.roll(x, s, axis=1)


def kernel_a(
    layers, kmt_ref, baro_ref,
    q_out, a2d_out, baro_out, col_out, row_out,
    uv, s, p, q, cuv, cs,
    m_uv, r_uv, m_p, r_p, m_s, r_s, m_q, r_q,
    d4, corr,
    b1, m1, r1, b2, m2, r2, a0v, r_a0v, r_rows, r_qrows,
    eta, ua, vv, dvv, da, dv, c2, c2a, cfa, cfv, sa, sv,
    load_sem, out_sem, send_sem, recv_sem,
):
    lon = lax.axis_index("lon")
    lat = lax.axis_index("lat")
    nlon = lax.axis_size("lon")
    nlat = lax.axis_size("lat")
    east = lax.rem(lon + 1, nlon)
    west = lax.rem(lon + nlon - 1, nlon)
    north = lax.rem(lat + 1, nlat)
    south = lax.rem(lat + nlat - 1, nlat)
    x_of = {-1: west, 0: lon, 1: east}
    y_of = {-1: south, 0: lat, 1: north}

    loads = {}
    n_load = 0
    for f in range(2):
        cp = pltpu.make_async_copy(layers.at[f], uv.at[f, :, 8:40, :], load_sem.at[n_load])
        cp.start()
        loads["uv", f] = cp
        n_load += 1
    for c in range(4):
        cp = pltpu.make_async_copy(
            layers.at[2:5, c * CH:(c + 1) * CH], s.at[0:3, c * CH:(c + 1) * CH], load_sem.at[n_load])
        cp.start()
        loads["s", c] = cp
        n_load += 1
    cp = pltpu.make_async_copy(layers.at[5], s.at[3], load_sem.at[n_load])
    cp.start()
    loads["age"] = cp

    barrier = pltpu.get_barrier_semaphore()
    around = [(dx, dy) for dx in (-1, 0, 1) for dy in (-1, 0, 1) if (dx, dy) != (0, 0)]
    for dx, dy in around:
        pl.semaphore_signal(barrier, inc=1, device_id=(x_of[dx], y_of[dy]), device_id_type=MESH)

    copies = {}

    def send(name, src, dst, dx, dy):
        at = len(copies)
        cp = pltpu.make_async_remote_copy(
            src_ref=src, dst_ref=dst, send_sem=send_sem.at[at], recv_sem=recv_sem.at[at],
            device_id=(x_of[dx], y_of[dy]), device_id_type=MESH)
        cp.start()
        copies[name] = cp

    lane = lanes()
    quad = lane >> 2
    in_quad = lane & 3
    kmt = kmt_ref[...]
    cmask = (kmt > 0).astype(F32)

    b1[1, 40:72, :] = baro_ref[1] * cmask
    b1[2, 40:72, :] = baro_ref[2] * cmask
    b1[3, 40:72, :] = kmt.astype(F32)

    for f in range(2):
        loads["uv", f].wait()

        def body(j, acc, f=f):
            xs = []
            for c in range(4):
                k = c * CH + j
                xs.append(jnp.where(k < kmt, uv[f, k, 8:40, :], 0.0))
            sel = quad == j
            out = []
            for c in range(4):
                out.append(jnp.where(sel, roll(xs[c], 4 * j + 2), acc[c]))
            for c in range(4):
                uv[f, c * CH + j, 8:40, :] = xs[c]
            return tuple(out)

        zero = jnp.zeros((R, C), F32)
        acc = lax.fori_loop(0, CH, body, (zero,) * 4)
        for c in range(4):
            cuv[f, c, 8:40, :] = acc[c]

    for c in range(4):
        cu, cv = cuv[0, c, 8:40, :], cuv[1, c, 8:40, :]
        m_uv[0, c] = jnp.where(in_quad < 2, cu, roll(cv, 2))
        m_uv[1, c] = jnp.where(in_quad < 2, roll(cu, -2), cv)

    pl.semaphore_wait(barrier, 8)

    send("uv_n", uv.at[:, :, 38:40, :], uv.at[:, :, 6:8, :], 0, 1)
    send("uv_s", uv.at[:, :, 8:10, :], uv.at[:, :, 40:42, :], 0, -1)
    for d, dx in ((0, 1), (1, -1)):
        send(("uv", dx, 0), m_uv.at[d], r_uv.at[d, :, 8:40, :], dx, 0)
        send(("uv", dx, 1), m_uv.at[d, :, 24:32, :], r_uv.at[d, :, 0:8, :], dx, 1)
        send(("uv", dx, -1), m_uv.at[d, :, 0:8, :], r_uv.at[d, :, 40:48, :], dx, -1)
    send("cuv_n", cuv.at[:, :, 32:40, :], cuv.at[:, :, 0:8, :], 0, 1)
    send("cuv_s", cuv.at[:, :, 8:16, :], cuv.at[:, :, 40:48, :], 0, -1)

    zero = jnp.zeros((R, C), F32)
    csum, total = zero, zero
    for c in range(4):
        loads["s", c].wait()

        def body(j, carry, c=c):
            csum, total, acc = carry
            k = c * CH + j
            m = k < kmt
            h = jnp.where(m, s[0, k], 0.0)
            w = ((GRAV * HALINE) * s[2, k] - (GRAV * THERMAL) * s[1, k]) * h
            pk = csum + 0.5 * w
            p[k, 8:40, :] = pk
            acc = jnp.where(quad == j, roll(pk, 4 * j + 2), acc)
            return csum + w, total + h, acc

        csum, total, acc = lax.fori_loop(0, CH, body, (csum, total, zero))
        cs[0, c] = acc

    def compact(field, lane_from):
        out = roll(cs[field, 0], -lane_from)
        for c in range(1, 4):
            out = jnp.where(in_quad == c, roll(cs[field, c], c - lane_from), out)
        return out

    m_p[0] = compact(0, 1)
    m_p[1] = compact(0, 2)
    b1[0, 40:72, :] = total * (1.0 / K)

    def side(fields, eastward):
        out = None
        for n, x in enumerate(fields):
            moved = roll(x, 32 * n + 32) if eastward else roll(x, 32 * n)
            out = moved if out is None else jnp.where(lane < 32 * n, out, moved)
        return out

    def unside(n, d):
        return (roll(d[0], 96 - 32 * n), roll(d[1], -32 * n))

    mine = [b1[n, 40:72, :] for n in range(3)]
    m1[0] = side(mine, True)
    m1[1] = side(mine, False)

    def send_sides(tag, m, r):
        for d, dx in ((0, 1), (1, -1)):
            send((tag, dx, 0), m.at[d], r.at[d, 32:64, :], dx, 0)
            send((tag, dx, 1), m.at[d], r.at[d, 0:32, :], dx, 1)
            send((tag, dx, -1), m.at[d], r.at[d, 64:96, :], dx, -1)

    send("p_e", m_p.at[0], r_p.at[0], 1, 0)
    send("p_w", m_p.at[1], r_p.at[1], -1, 0)
    send("p_n", p.at[:, 39, :], p.at[:, 7, :], 0, 1)
    send("p_s", p.at[:, 8, :], p.at[:, 40, :], 0, -1)
    send("b1_n", b1.at[:, 40:72, :], b1.at[:, 8:40, :], 0, 1)
    send("b1_s", b1.at[:, 40:72, :], b1.at[:, 72:104, :], 0, -1)
    send_sides("b1", m1, r1)

    loads["age"].wait()
    for f in range(4):

        def body(j, acc, f=f):
            sel = quad == j
            out = []
            for c in range(4):
                k = c * CH + j
                x = jnp.where(k < kmt, s[f, k], 0.0)
                out.append(jnp.where(sel, roll(x, 4 * j + 2), acc[c]))
            return tuple(out)

        acc = lax.fori_loop(0, CH, body, (zero,) * 4)
        for c in range(4):
            cs[1 + f, c] = acc[c]
        m_s[0, f] = compact(1 + f, 1)
        m_s[1, f] = compact(1 + f, 2)
    send("s_e", m_s.at[0], r_s.at[0], 1, 0)
    send("s_w", m_s.at[1], r_s.at[1], -1, 0)
    send("s_n", s.at[:, :, 31, :], r_rows.at[0], 0, 1)
    send("s_s", s.at[:, :, 0, :], r_rows.at[1], 0, -1)

    for name in ("b1_n", "b1_s"):
        copies[name].wait_recv()
    for dx in (1, -1):
        for dy in (0, 1, -1):
            copies["b1", dx, dy].wait_recv()
    for ref in (eta, dvv):
        for t in range(2):
            ref[t, 0:8, :] = jnp.zeros((8, C), F32)
            ref[t, 104:112, :] = jnp.zeros((8, C), F32)

    def tiles_of(n, centre, r, at):
        lo, hi = at
        t0 = centre[n, 8 + lo:8 + hi, :]
        from_west, from_east = unside(n, (r[0, lo:hi, :], r[1, lo:hi, :]))
        t1 = jnp.where(lane < 32, from_east, jnp.where(lane >= 96, from_west, 0.0))
        return t0, t1

    def shift_west(t0, t1):
        a, b = roll(t0, 1), roll(t1, 1)
        return jnp.where(lane < 1, b, a), jnp.where(lane < 1, a, b)

    for blk in range(3):
        at = (32 * blk, 32 * blk + 32)
        here = slice(8 + 32 * blk, 40 + 32 * blk)
        dd = tiles_of(0, b1, r1, at)
        uu = tiles_of(1, b1, r1, at)
        ww = tiles_of(2, b1, r1, at)
        dda = shift_west(*dd)
        uua = shift_west(*uu)
        for t in range(2):
            da[t, here, :] = dda[t]
            ua[t, here, :] = uua[t]
            dv[t, here, :] = dd[t]
            vv[t, here, :] = ww[t]
            dvv[t, here, :] = dd[t] * ww[t]
            c2[t, here, :] = jnp.where(dd[t] > 0.0, 0.5 * TAU, 0.0)
            c2a[t, here, :] = jnp.where(dda[t] > 0.0, 0.5 * TAU, 0.0)

    def next_height(lo, both):
        n = 2 if both else 1
        at = pl.ds(lo, 8)
        x = [da[t, at, :] * ua[t, at, :] for t in range(2)]
        r = [roll(x[t], -2) for t in range(2)]
        out = []
        for t in range(n):
            diff = jnp.where(lane < 126, r[t], r[1 - t]) - x[t]
            diff = diff + (dvv[t, pl.ds(lo + 1, 8), :] - dvv[t, pl.ds(lo - 1, 8), :])
            out.append(c2[t, at, :] * diff)
        return out

    for i in range(4):
        drop = next_height(40 + 8 * i, False)[0]
        b2[2, 40 + 8 * i:48 + 8 * i, :] = (
            baro_ref[0, 8 * i:8 * i + 8, :] * cmask[8 * i:8 * i + 8] - drop)

    for name in ("cuv_n", "cuv_s"):
        copies[name].wait_recv()
    for dx in (1, -1):
        for dy in (0, 1, -1):
            copies["uv", dx, dy].wait_recv()
    for c in range(4):
        w, e = r_uv[0, c], r_uv[1, c]
        d4[0, c] = jnp.where(in_quad < 2, w, roll(e, 2)) - cuv[0, c]
        d4[1, c] = jnp.where(in_quad < 2, roll(w, -2), e) - cuv[1, c]
    copies["p_e"].wait_recv()
    copies["p_w"].wait_recv()
    p_w, p_e = r_p[0], r_p[1]
    for c in range(4):
        for f in range(2):
            x = d4[f, c, 8:40, :]
            g = 2.0 * (d4[f, c, 9:41, :] + d4[f, c, 7:39, :]) - 8.0 * x
            out = jnp.where(in_quad < 2, roll(x, -2), roll(x, 2))
            out = out + jnp.where(in_quad == 1, roll(g, -1), jnp.where(in_quad == 2, roll(g, 1), 0.0))
            out = -NU * out
            if f == 0:
                own = cs[0, c]
                at_127 = 0.5 * (roll(own, -1) - roll(p_e, 1 - c))
                at_0 = 0.5 * (roll(p_w, 2 - c) - roll(own, 1))
                out = out + jnp.where(in_quad == 1, at_127, jnp.where(in_quad == 2, at_0, 0.0))
            corr[f, c] = out

    for name in ("uv_n", "uv_s", "p_n", "p_s"):
        copies[name].wait_recv()

    row = sublanes((R, C)) + lat * R
    cor = ROT * (2.0 * (row.astype(F32) + 0.5) / NY - 1.0)
    edge4 = (lane >= 126) | (lane < 2)

    def bilaplace(f, k):
        x = uv[f, k, 8:40, :]
        a = uv[f, k, 9:41, :] + uv[f, k, 7:39, :]
        b = uv[f, k, 10:42, :] + uv[f, k, 6:38, :]
        t = 2.0 * a - 8.0 * x
        e = roll(roll(x, -1) + t, -1)
        w = roll(roll(x, 1) + t, 1)
        return x, e + w + (b - 4.0 * t - 12.0 * x)

    sums = (zero,) * 4
    for c in range(4):

        def body(j, carry, c=c):
            sgu, sgv, squ, sqv, acc = carry
            k = c * CH + j
            m = k < kmt
            u0, lu = bilaplace(0, k)
            v0, lv = bilaplace(1, k)
            pk = p[k, 8:40, :]
            back = lax.rem(126 + C - 4 * j, C)
            cu = jnp.where(edge4, roll(corr[0, c], back), 0.0)
            cv = jnp.where(edge4, roll(corr[1, c], back), 0.0)
            gu = cor * v0 - NU * lu - 0.5 * (roll(pk, -1) - roll(pk, 1)) + cu
            gv = cv - cor * u0 - NU * lv - 0.5 * (p[k, 9:41, :] - p[k, 7:39, :])
            gu = jnp.where(m, gu, 0.0)
            gv = jnp.where(m, gv, 0.0)
            qu = u0 + DT * gu
            qv = v0 + DT * gv
            q[0, k] = qu
            q[1, k] = qv
            h = s[0, k]
            acc = jnp.where(quad == j, roll(qu, 4 * j + 2), acc)
            return sgu + gu * h, sgv + gv * h, squ + qu * h, sqv + qv * h, acc

        *sums, acc = lax.fori_loop(0, CH, body, (*sums, zero))
        cs[0, c] = acc
    sgu, sgv, squ, sqv = sums

    out_copies = []
    for f in range(2):
        cp = pltpu.make_async_copy(q.at[f], q_out.at[f], out_sem.at[f])
        cp.start()
        out_copies.append(cp)

    bound = jnp.maximum(total, 1.0)
    fu, fv = sgu / bound, sgv / bound
    a0u = -DT * fu - (squ - DT * fu * total) / bound
    a0v[...] = -DT * fv - (sqv - DT * fv * total) / bound
    b2[0, 40:72, :] = fu
    b2[1, 40:72, :] = fv
    mine = [fu, fv, b2[2, 40:72, :], a0u]
    m2[0] = side(mine, True)
    m2[1] = side(mine, False)
    send("b2_n", b2.at[:, 40:72, :], b2.at[:, 8:40, :], 0, 1)
    send("b2_s", b2.at[:, 40:72, :], b2.at[:, 72:104, :], 0, -1)
    send_sides("b2", m2, r2)
    send("a_n", a0v.at[24:32, :], r_a0v.at[0], 0, 1)
    send("a_s", a0v.at[0:8, :], r_a0v.at[1], 0, -1)
    m_q[0] = compact(0, 1)
    m_q[1] = compact(0, 2)
    send("q_e", m_q.at[0], r_q.at[0], 1, 0)
    send("q_w", m_q.at[1], r_q.at[1], -1, 0)
    send("q_n", q.at[1, :, 31, :], r_qrows.at[0], 0, 1)
    send("q_s", q.at[1, :, 0, :], r_qrows.at[1], 0, -1)

    for name in ("b2_n", "b2_s"):
        copies[name].wait_recv()
    for dx in (1, -1):
        for dy in (0, 1, -1):
            copies["b2", dx, dy].wait_recv()
    for blk in range(3):
        at = (32 * blk, 32 * blk + 32)
        here = slice(8 + 32 * blk, 40 + 32 * blk)
        ffu = shift_west(*tiles_of(0, b2, r2, at))
        ffv = tiles_of(1, b2, r2, at)
        ee = tiles_of(2, b2, r2, at)
        for t in range(2):
            eta[t, here, :] = ee[t]
            cfa[t, here, :] = 2.0 * c2a[t, here, :] * ffu[t]
            cfv[t, here, :] = 2.0 * c2[t, here, :] * ffv[t]

    sa[...] = jnp.zeros((2, R, C), F32)
    sv[...] = jnp.zeros((48, C), F32)

    def flows(first, count):
        for i in range(count):
            lo = 8 + 8 * (first + i)
            at = slice(lo, lo + 8)
            e = [eta[t, at, :] for t in range(2)]
            r = [roll(e[t], 2) for t in range(2)]
            for t in range(2):
                diff = e[t] - jnp.where(lane < 2, r[1 - t], r[t])
                new_u = ua[t, at, :] + (cfa[t, at, :] - c2a[t, at, :] * diff)
                ua[t, at, :] = new_u
                diff = eta[t, lo + 1:lo + 9, :] - eta[t, lo - 1:lo + 7, :]
                new_v = vv[t, at, :] + (cfv[t, at, :] - c2[t, at, :] * diff)
                vv[t, at, :] = new_v
                dvv[t, at, :] = dv[t, at, :] * new_v
                if 40 <= lo < 72:
                    sa[t, lo - 40:lo - 32, :] += new_u
                if t == 0 and 32 <= lo < 80:
                    sv[lo - 32:lo - 24, :] += new_v

    def heights(first, count):
        for i in range(count):
            lo = 8 + 8 * (first + i)
            drop = next_height(lo, True)
            for t in range(2):
                eta[t, lo:lo + 8, :] = eta[t, lo:lo + 8, :] - drop[t]

    flows(0, 12)
    for group in range(4):
        first, count = group, 12 - 2 * group

        def body(n, carry, first=first, count=count):
            heights(first, count)
            flows(first, count)
            return carry

        lax.fori_loop(0, 3 if group == 0 else 4, body, 0)

    sa0, sa1 = sa[0], sa[1]
    su = jnp.where(lane < 127, roll(sa0, -1), roll(sa1, -1))
    a2d_out[0] = a0u + su * (1.0 / NSUB)
    a2d_out[1] = a0v[...] + sv[8:40, :] * (1.0 / NSUB)
    baro_out[0] = eta[0, 40:72, :]
    baro_out[1] = jnp.where(lane < 127, roll(ua[0, 40:72, :], -1), roll(ua[1, 40:72, :], -1))
    baro_out[2] = vv[0, 40:72, :]

    for name in ("s_e", "s_w", "q_e", "q_w"):
        copies[name].wait_recv()
    a_w = r2[0, 32:64, 127:128] + sa0[:, 0:1] * (1.0 / NSUB)
    a_e = r2[1, 32:64, 96:97] + sa1[:, 1:2] * (1.0 / NSUB)
    halves = []
    for d, a, sign in ((0, a_w, 1.0), (1, a_e, -1.0)):
        flux = (0.5 * DT) * r_s[d, 0] * (r_q[d] + a)
        vals = [flux]
        for n in range(1, 4):
            vals.append(r_s[d, n] * ((DT * KAPPA) + sign * flux))
        halves.append(vals)
    for n in range(4):
        w, e = halves[0][n], halves[1][n]
        col_out[n, 0] = jnp.where(
            in_quad == 0, e, jnp.where(in_quad == 1, roll(w, 1), jnp.where(in_quad == 2, roll(e, 1), roll(w, 2))))
        col_out[n, 1] = jnp.where(
            in_quad == 0, roll(e, -2), jnp.where(in_quad == 1, roll(w, -1), jnp.where(in_quad == 2, roll(e, -1), w)))

    for name in ("s_n", "s_s", "q_n", "q_s", "a_n", "a_s"):
        copies[name].wait_recv()
    level = sublanes((K, C)).astype(F32)
    for d, kmt_row, a_row, sign in (
        (0, b1[3, 39:40, :], r_a0v[0, 7:8, :] + sv[7:8, :] * (1.0 / NSUB), 1.0),
        (1, b1[3, 72:73, :], r_a0v[1, 0:1, :] + sv[40:41, :] * (1.0 / NSUB), -1.0),
    ):
        m = level < kmt_row
        flux = jnp.where(m, (0.5 * DT) * r_rows[d, 0] * (r_qrows[d] + a_row), 0.0)
        row_out[4 * d] = flux
        for n in range(1, 4):
            row_out[4 * d + n] = jnp.where(m, r_rows[d, n], 0.0) * ((DT * KAPPA) + sign * flux)

    for cp in copies.values():
        cp.wait_send()
    for cp in out_copies:
        cp.wait()


N_COPIES = 2 + 6 + 2 + 4 + 2 + 6 + 4 + 2 + 6 + 2 + 4


def call_a(layers, kmt, baro):
    v = lambda *shape: pltpu.VMEM(shape, F32)
    surface = [v(2, 112, C) for _ in range(10)]
    return pl.pallas_call(
        kernel_a,
        out_shape=(
            jax.ShapeDtypeStruct((2, K, R, C), F32),
            jax.ShapeDtypeStruct((2, R, C), F32),
            jax.ShapeDtypeStruct((3, R, C), F32),
            jax.ShapeDtypeStruct((4, 2, R, C), F32),
            jax.ShapeDtypeStruct((8, K, C), F32),
        ),
        in_specs=[
            pl.BlockSpec(memory_space=pl.ANY),
            pl.BlockSpec(memory_space=pltpu.VMEM),
            pl.BlockSpec(memory_space=pltpu.VMEM),
        ],
        out_specs=(
            pl.BlockSpec(memory_space=pl.ANY),
            pl.BlockSpec(memory_space=pltpu.VMEM),
            pl.BlockSpec(memory_space=pltpu.VMEM),
            pl.BlockSpec(memory_space=pltpu.VMEM),
            pl.BlockSpec(memory_space=pltpu.VMEM),
        ),
        scratch_shapes=[
            v(2, K, 48, C), v(4, K, R, C), v(K, 48, C), v(2, K, R, C), v(2, 4, 48, C), v(5, 4, R, C),
            v(2, 4, R, C), v(2, 4, 48, C), v(2, R, C), v(2, R, C), v(2, 4, R, C), v(2, 4, R, C), v(2, R, C), v(2, R, C),
            v(2, 4, 48, C), v(2, 4, R, C),
            v(4, 112, C), v(2, R, C), v(2, 96, C), v(3, 112, C), v(2, R, C), v(2, 96, C),
            v(R, C), v(2, 8, C), v(2, 4, K, C), v(2, K, C),
            *surface, v(2, R, C), v(48, C),
            pltpu.SemaphoreType.DMA((7,)),
            pltpu.SemaphoreType.DMA((2,)),
            pltpu.SemaphoreType.DMA((N_COPIES,)),
            pltpu.SemaphoreType.DMA((N_COPIES,)),
        ],
        compiler_params=pltpu.CompilerParams(
            collective_id=0, has_side_effects=True, vmem_limit_bytes=50 * 2**20),
        name="tendencies_and_surface",
    )(layers, kmt, baro)


LB = 10


def kernel_b(ht, sa, q, a2d, kmt_ref, col, rows, baro, out, baro_out):
    step = pl.program_id(0)
    lane = lanes()
    sub = sublanes((8, C))
    kmt = kmt_ref[...]
    au, av = a2d[0], a2d[1]
    kd = DT * KAPPA

    @pl.when(step == 0)
    def _():
        baro_out[...] = baro[...]

    def tiles(x):
        return [x[8 * i:8 * i + 8] for i in range(4)]

    def from_north(x, halo):
        r = [pltpu.roll(t, 7, axis=0) for t in tiles(x)] + [jnp.broadcast_to(halo, (8, C))]
        return jnp.concatenate([jnp.where(sub == 7, r[i + 1], r[i]) for i in range(4)], axis=0)

    def from_south(x, halo):
        r = [jnp.broadcast_to(halo, (8, C))] + [pltpu.roll(t, 1, axis=0) for t in tiles(x)]
        return jnp.concatenate([jnp.where(sub == 0, r[i], r[i + 1]) for i in range(4)], axis=0)

    def body(l, carry):
        k = step * LB + l
        c = k // CH
        j = k - c * CH
        tile = k // (2 * CH)
        back = 127 - 4 * j - 2 * (c - 2 * tile)
        m = k < kmt
        h = ht[0, l]
        un = jnp.where(m, q[0, l] + au, 0.0)
        vn = jnp.where(m, q[1, l] + av, 0.0)
        out[0, l] = un
        out[1, l] = vn
        h5 = (0.5 * DT) * h
        fu, fv = h5 * un, h5 * vn

        def halo(n):
            return roll(col[n, tile], back)

        def row_n(n):
            return rows[4 + n, pl.ds(k, 1), :]

        def row_s(n):
            return rows[n, pl.ds(k, 1), :]

        hal = halo(0)
        e = jnp.where(lane == 127, hal, roll(fu, -1))
        w = jnp.where(lane == 0, hal, roll(fu, 1))
        hn = h - ((e - w) + (from_north(fv, row_n(0)) - from_south(fv, row_s(0))))
        out[2, l] = jnp.where(m, hn, 0.0)
        ke, kw, kn, ks = kd - fu, kd + fu, kd - fv, kd + fv
        mid = h - 4.0 * kd
        for n, (ref, at) in enumerate(((ht, 1), (sa, 0), (sa, 1)), start=1):
            x = jnp.where(m, ref[at, l], 0.0)
            hal = halo(n)
            e = jnp.where(lane == 127, hal, roll(x * ke, -1))
            w = jnp.where(lane == 0, hal, roll(x * kw, 1))
            r = from_north(x * kn, row_n(n)) + from_south(x * ks, row_s(n))
            out[2 + n, l] = jnp.where(m, (e + w) + (r + x * mid), 0.0)
        return carry

    lax.fori_loop(0, LB, body, 0)


def call_b(layers, q, a2d, kmt, col, rows, baro):
    whole = lambda *shape: pl.BlockSpec(shape, lambda i: (0,) * len(shape))
    return pl.pallas_call(
        kernel_b,
        grid=(K // LB,),
        out_shape=(
            jax.ShapeDtypeStruct((6, K, R, C), F32),
            jax.ShapeDtypeStruct((3, R, C), F32),
        ),
        in_specs=[
            pl.BlockSpec((2, LB, R, C), lambda i: (1, i, 0, 0)),
            pl.BlockSpec((2, LB, R, C), lambda i: (2, i, 0, 0)),
            pl.BlockSpec((2, LB, R, C), lambda i: (0, i, 0, 0)),
            whole(2, R, C), whole(R, C), whole(4, 2, R, C), whole(8, K, C), whole(3, R, C),
        ],
        out_specs=(
            pl.BlockSpec((6, LB, R, C), lambda i: (0, i, 0, 0)),
            whole(3, R, C),
        ),
        compiler_params=pltpu.CompilerParams(vmem_limit_bytes=40 * 2**20),
        name="transport",
    )(layers, layers, q, a2d, kmt, col, rows, baro)


def per_device(layers, kmt, barotropic):
    q, a2d, baro, col, rows = call_a(layers, kmt, barotropic)
    return call_b(layers, q, a2d, kmt, col, rows, baro)


def solution(mesh):
    return jax.shard_map(
        per_device,
        mesh=mesh,
        in_specs=(P(None, None, "lat", "lon"), P("lat", "lon"), P(None, "lat", "lon")),
        out_specs=(P(None, None, "lat", "lon"), P(None, "lat", "lon")),
        check_vma=False,
    )
```

```python
import jax
import jax.numpy as jnp
from jax import lax
from jax.experimental import pallas as pl
from jax.experimental.pallas import tpu as pltpu
from jax.sharding import PartitionSpec as P

K = 100
NSUB = 16
R = 32
C = 128
CH = 25
UNROLL = 5
NY = 256

DT = 0.1
TAU = 0.6
NU = 0.01
KAPPA = 0.1
GRAV = 0.1
THERMAL = 1.0
HALINE = 0.8
ROT = 0.5

F32 = jnp.float32
MESH = pl.DeviceIdType.MESH


def lanes(shape=(1, C)):
    return lax.broadcasted_iota(jnp.int32, shape, 1)


def sublanes(shape):
    return lax.broadcasted_iota(jnp.int32, shape, 0)


def roll(x, s):
    if isinstance(s, int):
        s %= C
        if s == 0:
            return x
    return pltpu.roll(x, s, axis=1)


def kernel_a(
    layers, kmt_hbm, baro_hbm,
    q, s, kmt_ref, a2d_out, baro_out, col_out, row_out,
    uv, p, baro_ref, cuv, cs,
    m_uv, r_uv, m_p, r_p, m_s, r_s, m_q, r_q,
    d4, corr,
    b1, m1, r1, b2, m2, r2, a0v, r_a0v, r_rows, r_qrows,
    eta, ua, vv, dvv, da, dv, c2, c2a, cfa, cfv, sa, sv,
    load_sem, send_sem, recv_sem,
):
    lon = lax.axis_index("lon")
    lat = lax.axis_index("lat")
    nlon = lax.axis_size("lon")
    nlat = lax.axis_size("lat")
    east = lax.rem(lon + 1, nlon)
    west = lax.rem(lon + nlon - 1, nlon)
    north = lax.rem(lat + 1, nlat)
    south = lax.rem(lat + nlat - 1, nlat)
    x_of = {-1: west, 0: lon, 1: east}
    y_of = {-1: south, 0: lat, 1: north}

    loads = {}
    n_load = 0
    for name, src, dst in (("kmt", kmt_hbm, kmt_ref), ("baro", baro_hbm, baro_ref)):
        cp = pltpu.make_async_copy(src, dst, load_sem.at[n_load])
        cp.start()
        loads[name] = cp
        n_load += 1
    for f in range(2):
        cp = pltpu.make_async_copy(layers.at[f], uv.at[f, :, 8:40, :], load_sem.at[n_load])
        cp.start()
        loads["uv", f] = cp
        n_load += 1
    for c in range(4):
        cp = pltpu.make_async_copy(
            layers.at[2:5, c * CH:(c + 1) * CH], s.at[0:3, c * CH:(c + 1) * CH], load_sem.at[n_load])
        cp.start()
        loads["s", c] = cp
        n_load += 1
    cp = pltpu.make_async_copy(layers.at[5], s.at[3], load_sem.at[n_load])
    cp.start()
    loads["age"] = cp

    barrier = pltpu.get_barrier_semaphore()
    around = [(dx, dy) for dx in (-1, 0, 1) for dy in (-1, 0, 1) if (dx, dy) != (0, 0)]
    for dx, dy in around:
        pl.semaphore_signal(barrier, inc=1, device_id=(x_of[dx], y_of[dy]), device_id_type=MESH)

    copies = {}

    def send(name, src, dst, dx, dy):
        at = len(copies)
        cp = pltpu.make_async_remote_copy(
            src_ref=src, dst_ref=dst, send_sem=send_sem.at[at], recv_sem=recv_sem.at[at],
            device_id=(x_of[dx], y_of[dy]), device_id_type=MESH)
        cp.start()
        copies[name] = cp

    lane = lanes()
    quad = lane >> 2
    in_quad = lane & 3
    loads["kmt"].wait()
    loads["baro"].wait()
    kmt = kmt_ref[...]
    cmask = (kmt > 0).astype(F32)

    b1[1, 40:72, :] = baro_ref[1] * cmask
    b1[2, 40:72, :] = baro_ref[2] * cmask
    b1[3, 40:72, :] = kmt.astype(F32)

    def pack(fields, store=False):
        def body(j, accs):
            sel = quad == j
            out = []
            xs = {}
            for f, (load, masked, _) in enumerate(fields):
                for c in range(4):
                    k = c * CH + j
                    x = load(k)
                    xs[f, c] = jnp.where(k < kmt, x, 0.0) if masked else x
            for f in range(len(fields)):
                for c in range(4):
                    out.append(jnp.where(sel, roll(xs[f, c], 4 * j + 2), accs[4 * f + c]))
            if store:
                for f in range(len(fields)):
                    for c in range(4):
                        uv[f, c * CH + j, 8:40, :] = xs[f, c]
            return tuple(out)

        accs = lax.fori_loop(0, CH, body, (jnp.zeros((R, C), F32),) * (4 * len(fields)), unroll=UNROLL)
        for f, (_, _, put) in enumerate(fields):
            for c in range(4):
                put(c, accs[4 * f + c])

    def put_cuv(f):
        def put(c, x):
            cuv[f, c, 8:40, :] = x
        return put

    def put_cs(f):
        def put(c, x):
            cs[f, c] = x
        return put

    loads["uv", 0].wait()
    loads["uv", 1].wait()
    pack([(lambda k, f=f: uv[f, k, 8:40, :], True, put_cuv(f)) for f in range(2)], store=True)

    for c in range(4):
        cu, cv = cuv[0, c, 8:40, :], cuv[1, c, 8:40, :]
        m_uv[0, c] = jnp.where(in_quad < 2, cu, roll(cv, 2))
        m_uv[1, c] = jnp.where(in_quad < 2, roll(cu, -2), cv)

    pl.semaphore_wait(barrier, 8)

    send("uv_n", uv.at[:, :, 38:40, :], uv.at[:, :, 6:8, :], 0, 1)
    send("uv_s", uv.at[:, :, 8:10, :], uv.at[:, :, 40:42, :], 0, -1)
    for d, dx in ((0, 1), (1, -1)):
        send(("uv", dx, 0), m_uv.at[d], r_uv.at[d, :, 8:40, :], dx, 0)
        send(("uv", dx, 1), m_uv.at[d, :, 24:32, :], r_uv.at[d, :, 0:8, :], dx, 1)
        send(("uv", dx, -1), m_uv.at[d, :, 0:8, :], r_uv.at[d, :, 40:48, :], dx, -1)
    send("cuv_n", cuv.at[:, :, 32:40, :], cuv.at[:, :, 0:8, :], 0, 1)
    send("cuv_s", cuv.at[:, :, 8:16, :], cuv.at[:, :, 40:48, :], 0, -1)

    zero = jnp.zeros((R, C), F32)
    csum, total = zero, zero
    for c in range(4):
        loads["s", c].wait()

        def body(j, carry, c=c):
            csum, total = carry
            k = c * CH + j
            m = k < kmt
            h = jnp.where(m, s[0, k], 0.0)
            w = ((GRAV * HALINE) * s[2, k] - (GRAV * THERMAL) * s[1, k]) * h
            pk = csum + 0.5 * w
            p[k, 8:40, :] = pk
            return csum + w, total + h

        csum, total = lax.fori_loop(0, CH, body, (csum, total), unroll=UNROLL)
    pack([(lambda k: p[k, 8:40, :], False, put_cs(0))])

    def compact(field, lane_from):
        out = roll(cs[field, 0], -lane_from)
        for c in range(1, 4):
            out = jnp.where(in_quad == c, roll(cs[field, c], c - lane_from), out)
        return out

    m_p[0] = compact(0, 1)
    m_p[1] = compact(0, 2)
    b1[0, 40:72, :] = total * (1.0 / K)

    def side(fields, eastward):
        out = None
        for n, x in enumerate(fields):
            moved = roll(x, 32 * n + 32) if eastward else roll(x, 32 * n)
            out = moved if out is None else jnp.where(lane < 32 * n, out, moved)
        return out

    def unside(n, d):
        return (roll(d[0], 96 - 32 * n), roll(d[1], -32 * n))

    mine = [b1[n, 40:72, :] for n in range(3)]
    m1[0] = side(mine, True)
    m1[1] = side(mine, False)

    def send_sides(tag, m, r):
        for d, dx in ((0, 1), (1, -1)):
            send((tag, dx, 0), m.at[d], r.at[d, 32:64, :], dx, 0)
            send((tag, dx, 1), m.at[d], r.at[d, 0:32, :], dx, 1)
            send((tag, dx, -1), m.at[d], r.at[d, 64:96, :], dx, -1)

    send("p_e", m_p.at[0], r_p.at[0], 1, 0)
    send("p_w", m_p.at[1], r_p.at[1], -1, 0)
    send("p_n", p.at[:, 39, :], p.at[:, 7, :], 0, 1)
    send("p_s", p.at[:, 8, :], p.at[:, 40, :], 0, -1)
    send("b1_n", b1.at[:, 40:72, :], b1.at[:, 8:40, :], 0, 1)
    send("b1_s", b1.at[:, 40:72, :], b1.at[:, 72:104, :], 0, -1)
    send_sides("b1", m1, r1)

    def pack_scalars(which):
        pack([(lambda k, f=f: s[f, k], True, put_cs(1 + f)) for f in which])
        for f in which:
            m_s[0, f] = compact(1 + f, 1)
            m_s[1, f] = compact(1 + f, 2)

    pack_scalars((0, 1))
    loads["age"].wait()
    pack_scalars((2, 3))
    send("s_e", m_s.at[0], r_s.at[0], 1, 0)
    send("s_w", m_s.at[1], r_s.at[1], -1, 0)
    send("s_n", s.at[:, :, 31, :], r_rows.at[0], 0, 1)
    send("s_s", s.at[:, :, 0, :], r_rows.at[1], 0, -1)

    for name in ("b1_n", "b1_s"):
        copies[name].wait_recv()
    for dx in (1, -1):
        for dy in (0, 1, -1):
            copies["b1", dx, dy].wait_recv()
    for ref in (eta, dvv):
        for t in range(2):
            ref[t, 0:8, :] = jnp.zeros((8, C), F32)
            ref[t, 104:112, :] = jnp.zeros((8, C), F32)

    def tiles_of(n, centre, r, at):
        lo, hi = at
        t0 = centre[n, 8 + lo:8 + hi, :]
        from_west, from_east = unside(n, (r[0, lo:hi, :], r[1, lo:hi, :]))
        t1 = jnp.where(lane < 32, from_east, jnp.where(lane >= 96, from_west, 0.0))
        return t0, t1

    def shift_west(t0, t1):
        a, b = roll(t0, 1), roll(t1, 1)
        return jnp.where(lane < 1, b, a), jnp.where(lane < 1, a, b)

    for blk in range(3):
        at = (32 * blk, 32 * blk + 32)
        here = slice(8 + 32 * blk, 40 + 32 * blk)
        dd = tiles_of(0, b1, r1, at)
        uu = tiles_of(1, b1, r1, at)
        ww = tiles_of(2, b1, r1, at)
        dda = shift_west(*dd)
        uua = shift_west(*uu)
        for t in range(2):
            da[t, here, :] = dda[t]
            ua[t, here, :] = uua[t]
            dv[t, here, :] = dd[t]
            vv[t, here, :] = ww[t]
            dvv[t, here, :] = dd[t] * ww[t]
            c2[t, here, :] = jnp.where(dd[t] > 0.0, 0.5 * TAU, 0.0)
            c2a[t, here, :] = jnp.where(dda[t] > 0.0, 0.5 * TAU, 0.0)

    def next_height(lo, both):
        n = 2 if both else 1
        at = pl.ds(lo, 8)
        x = [da[t, at, :] * ua[t, at, :] for t in range(2)]
        r = [roll(x[t], -2) for t in range(2)]
        out = []
        for t in range(n):
            diff = jnp.where(lane < 126, r[t], r[1 - t]) - x[t]
            diff = diff + (dvv[t, pl.ds(lo + 1, 8), :] - dvv[t, pl.ds(lo - 1, 8), :])
            out.append(c2[t, at, :] * diff)
        return out

    for i in range(4):
        drop = next_height(40 + 8 * i, False)[0]
        b2[2, 40 + 8 * i:48 + 8 * i, :] = (
            baro_ref[0, 8 * i:8 * i + 8, :] * cmask[8 * i:8 * i + 8] - drop)

    for name in ("cuv_n", "cuv_s"):
        copies[name].wait_recv()
    for dx in (1, -1):
        for dy in (0, 1, -1):
            copies["uv", dx, dy].wait_recv()
    for c in range(4):
        w, e = r_uv[0, c], r_uv[1, c]
        d4[0, c] = jnp.where(in_quad < 2, w, roll(e, 2)) - cuv[0, c]
        d4[1, c] = jnp.where(in_quad < 2, roll(w, -2), e) - cuv[1, c]
    copies["p_e"].wait_recv()
    copies["p_w"].wait_recv()
    p_w, p_e = r_p[0], r_p[1]
    for c in range(4):
        for f in range(2):
            x = d4[f, c, 8:40, :]
            g = 2.0 * (d4[f, c, 9:41, :] + d4[f, c, 7:39, :]) - 8.0 * x
            out = jnp.where(in_quad < 2, roll(x, -2), roll(x, 2))
            out = out + jnp.where(in_quad == 1, roll(g, -1), jnp.where(in_quad == 2, roll(g, 1), 0.0))
            out = -NU * out
            if f == 0:
                own = cs[0, c]
                at_127 = 0.5 * (roll(own, -1) - roll(p_e, 1 - c))
                at_0 = 0.5 * (roll(p_w, 2 - c) - roll(own, 1))
                out = out + jnp.where(in_quad == 1, at_127, jnp.where(in_quad == 2, at_0, 0.0))
            corr[f, c] = out

    for name in ("uv_n", "uv_s", "p_n", "p_s"):
        copies[name].wait_recv()

    row = sublanes((R, C)) + lat * R
    cor = ROT * (2.0 * (row.astype(F32) + 0.5) / NY - 1.0)
    edge4 = (lane >= 126) | (lane < 2)

    def stencil(f, k):
        x = uv[f, k, 8:40, :]
        one = uv[f, k, 9:41, :] + uv[f, k, 7:39, :]
        two = uv[f, k, 10:42, :] + uv[f, k, 6:38, :]
        far = -NU * x
        near = (-2.0 * NU) * one - 8.0 * far
        return x, far, near, -NU * two - 4.0 * near - 12.0 * far

    sums = (zero,) * 4
    for c in range(4):

        def body(j, carry, c=c):
            sgu, sgv, squ, sqv, acc = carry
            k = c * CH + j
            m = k < kmt
            u0, ufar, unear, gu = stencil(0, k)
            v0, vfar, vnear, gv = stencil(1, k)
            hp = 0.5 * p[k, 8:40, :]
            back = lax.rem(126 + C - 4 * j, C)
            cu = roll(corr[0, c], back)
            cv = roll(corr[1, c], back)
            ue = roll(unear - hp, -1)
            uw = roll(unear + hp, 1)
            uee, uww = roll(ufar, -2), roll(ufar, 2)
            ve, vw = roll(vnear, -1), roll(vnear, 1)
            vee, vww = roll(vfar, -2), roll(vfar, 2)
            gu = gu + cor * v0
            gv = gv - cor * u0 - 0.5 * (p[k, 9:41, :] - p[k, 7:39, :])
            gu = gu + jnp.where(edge4, cu, 0.0) + ((ue + uw) + (uee + uww))
            gv = gv + jnp.where(edge4, cv, 0.0) + ((ve + vw) + (vee + vww))
            gu = jnp.where(m, gu, 0.0)
            gv = jnp.where(m, gv, 0.0)
            qu = u0 + DT * gu
            qv = v0 + DT * gv
            q[0, k] = qu
            q[1, k] = qv
            h = s[0, k]
            acc = jnp.where(quad == j, roll(qu, 4 * j + 2), acc)
            return sgu + gu * h, sgv + gv * h, squ + qu * h, sqv + qv * h, acc

        *sums, acc = lax.fori_loop(0, CH, body, (*sums, zero), unroll=UNROLL)
        cs[0, c] = acc
    sgu, sgv, squ, sqv = sums

    bound = jnp.maximum(total, 1.0)
    fu, fv = sgu / bound, sgv / bound
    a0u = -DT * fu - (squ - DT * fu * total) / bound
    a0v[...] = -DT * fv - (sqv - DT * fv * total) / bound
    b2[0, 40:72, :] = fu
    b2[1, 40:72, :] = fv
    mine = [fu, fv, b2[2, 40:72, :], a0u]
    m2[0] = side(mine, True)
    m2[1] = side(mine, False)
    send("b2_n", b2.at[:, 40:72, :], b2.at[:, 8:40, :], 0, 1)
    send("b2_s", b2.at[:, 40:72, :], b2.at[:, 72:104, :], 0, -1)
    send_sides("b2", m2, r2)
    send("a_n", a0v.at[24:32, :], r_a0v.at[0], 0, 1)
    send("a_s", a0v.at[0:8, :], r_a0v.at[1], 0, -1)
    m_q[0] = compact(0, 1)
    m_q[1] = compact(0, 2)
    send("q_e", m_q.at[0], r_q.at[0], 1, 0)
    send("q_w", m_q.at[1], r_q.at[1], -1, 0)
    send("q_n", q.at[1, :, 31, :], r_qrows.at[0], 0, 1)
    send("q_s", q.at[1, :, 0, :], r_qrows.at[1], 0, -1)

    for name in ("b2_n", "b2_s"):
        copies[name].wait_recv()
    for dx in (1, -1):
        for dy in (0, 1, -1):
            copies["b2", dx, dy].wait_recv()
    for blk in range(3):
        at = (32 * blk, 32 * blk + 32)
        here = slice(8 + 32 * blk, 40 + 32 * blk)
        ffu = shift_west(*tiles_of(0, b2, r2, at))
        ffv = tiles_of(1, b2, r2, at)
        ee = tiles_of(2, b2, r2, at)
        for t in range(2):
            eta[t, here, :] = ee[t]
            cfa[t, here, :] = 2.0 * c2a[t, here, :] * ffu[t]
            cfv[t, here, :] = 2.0 * c2[t, here, :] * ffv[t]

    sa[...] = jnp.zeros((2, R, C), F32)
    sv[...] = jnp.zeros((48, C), F32)

    def flows(first, count):
        for i in range(count):
            lo = 8 + 8 * (first + i)
            at = slice(lo, lo + 8)
            e = [eta[t, at, :] for t in range(2)]
            r = [roll(e[t], 2) for t in range(2)]
            for t in range(2):
                diff = e[t] - jnp.where(lane < 2, r[1 - t], r[t])
                new_u = ua[t, at, :] + (cfa[t, at, :] - c2a[t, at, :] * diff)
                ua[t, at, :] = new_u
                diff = eta[t, lo + 1:lo + 9, :] - eta[t, lo - 1:lo + 7, :]
                new_v = vv[t, at, :] + (cfv[t, at, :] - c2[t, at, :] * diff)
                vv[t, at, :] = new_v
                dvv[t, at, :] = dv[t, at, :] * new_v
                if 40 <= lo < 72:
                    sa[t, lo - 40:lo - 32, :] += new_u
                if t == 0 and 32 <= lo < 80:
                    sv[lo - 32:lo - 24, :] += new_v

    def heights(first, count):
        for i in range(count):
            lo = 8 + 8 * (first + i)
            drop = next_height(lo, True)
            for t in range(2):
                eta[t, lo:lo + 8, :] = eta[t, lo:lo + 8, :] - drop[t]

    flows(0, 12)
    for group in range(4):
        first, count = group, 12 - 2 * group

        def body(n, carry, first=first, count=count):
            heights(first, count)
            flows(first, count)
            return carry

        lax.fori_loop(0, 3 if group == 0 else 4, body, 0)

    sa0, sa1 = sa[0], sa[1]
    su = jnp.where(lane < 127, roll(sa0, -1), roll(sa1, -1))
    a2d_out[0] = a0u + su * (1.0 / NSUB)
    a2d_out[1] = a0v[...] + sv[8:40, :] * (1.0 / NSUB)
    baro_out[0] = eta[0, 40:72, :]
    baro_out[1] = jnp.where(lane < 127, roll(ua[0, 40:72, :], -1), roll(ua[1, 40:72, :], -1))
    baro_out[2] = vv[0, 40:72, :]

    for name in ("s_e", "s_w", "q_e", "q_w"):
        copies[name].wait_recv()
    a_w = r2[0, 32:64, 127:128] + sa0[:, 0:1] * (1.0 / NSUB)
    a_e = r2[1, 32:64, 96:97] + sa1[:, 1:2] * (1.0 / NSUB)
    halves = []
    for d, a, sign in ((0, a_w, 1.0), (1, a_e, -1.0)):
        flux = (0.5 * DT) * r_s[d, 0] * (r_q[d] + a)
        vals = [flux]
        for n in range(1, 4):
            vals.append(r_s[d, n] * ((DT * KAPPA) + sign * flux))
        halves.append(vals)
    for n in range(4):
        w, e = halves[0][n], halves[1][n]
        col_out[n, 0] = jnp.where(
            in_quad == 0, e, jnp.where(in_quad == 1, roll(w, 1), jnp.where(in_quad == 2, roll(e, 1), roll(w, 2))))
        col_out[n, 1] = jnp.where(
            in_quad == 0, roll(e, -2), jnp.where(in_quad == 1, roll(w, -1), jnp.where(in_quad == 2, roll(e, -1), w)))

    for name in ("s_n", "s_s", "q_n", "q_s", "a_n", "a_s"):
        copies[name].wait_recv()
    level = sublanes((K, C)).astype(F32)
    for d, kmt_row, a_row, sign in (
        (0, b1[3, 39:40, :], r_a0v[0, 7:8, :] + sv[7:8, :] * (1.0 / NSUB), 1.0),
        (1, b1[3, 72:73, :], r_a0v[1, 0:1, :] + sv[40:41, :] * (1.0 / NSUB), -1.0),
    ):
        m = level < kmt_row
        flux = jnp.where(m, (0.5 * DT) * r_rows[d, 0] * (r_qrows[d] + a_row), 0.0)
        row_out[4 * d] = flux
        for n in range(1, 4):
            row_out[4 * d + n] = jnp.where(m, r_rows[d, n], 0.0) * ((DT * KAPPA) + sign * flux)

    for cp in copies.values():
        cp.wait_send()


N_COPIES = 2 + 6 + 2 + 4 + 2 + 6 + 4 + 2 + 6 + 2 + 4


def call_a(layers, kmt, baro):
    v = lambda *shape: pltpu.VMEM(shape, F32)
    surface = [v(2, 112, C) for _ in range(10)]
    vmem = pl.BlockSpec(memory_space=pltpu.VMEM)
    shape = lambda *dims: jax.ShapeDtypeStruct(dims, F32)
    return pl.pallas_call(
        kernel_a,
        out_shape=(
            shape(2, K, R, C), shape(4, K, R, C), jax.ShapeDtypeStruct((R, C), jnp.int32),
            shape(2, R, C), shape(3, R, C), shape(4, 2, R, C), shape(8, K, C),
        ),
        in_specs=[pl.BlockSpec(memory_space=pltpu.HBM)] * 3,
        out_specs=(vmem,) * 7,
        scratch_shapes=[
            v(2, K, 48, C), v(K, 48, C), v(3, R, C), v(2, 4, 48, C), v(5, 4, R, C),
            v(2, 4, R, C), v(2, 4, 48, C), v(2, R, C), v(2, R, C), v(2, 4, R, C), v(2, 4, R, C), v(2, R, C), v(2, R, C),
            v(2, 4, 48, C), v(2, 4, R, C),
            v(4, 112, C), v(2, R, C), v(2, 96, C), v(3, 112, C), v(2, R, C), v(2, 96, C),
            v(R, C), v(2, 8, C), v(2, 4, K, C), v(2, K, C),
            *surface, v(2, R, C), v(48, C),
            pltpu.SemaphoreType.DMA((9,)),
            pltpu.SemaphoreType.DMA((N_COPIES,)),
            pltpu.SemaphoreType.DMA((N_COPIES,)),
        ],
        compiler_params=pltpu.CompilerParams(
            collective_id=0, has_side_effects=True, vmem_limit_bytes=42 * 2**20),
        name="tendencies_and_surface",
    )(layers, kmt, baro)


LB = 10


def kernel_b(q, s, kmt_ref, a2d, baro, col, rows, out_hbm, baro_hbm, out, out_sem):
    lane = lanes()
    sub = sublanes((8, C))
    kmt = kmt_ref[...]
    au, av = a2d[0], a2d[1]
    kd = DT * KAPPA

    copies = [pltpu.make_async_copy(baro, baro_hbm, out_sem.at[K // LB])]
    copies[0].start()

    def tiles(x):
        return [x[8 * i:8 * i + 8] for i in range(4)]

    def from_north(x, halo):
        r = [pltpu.roll(t, 7, axis=0) for t in tiles(x)] + [jnp.broadcast_to(halo, (8, C))]
        return jnp.concatenate([jnp.where(sub == 7, r[i + 1], r[i]) for i in range(4)], axis=0)

    def from_south(x, halo):
        r = [jnp.broadcast_to(halo, (8, C))] + [pltpu.roll(t, 1, axis=0) for t in tiles(x)]
        return jnp.concatenate([jnp.where(sub == 0, r[i], r[i + 1]) for i in range(4)], axis=0)

    def body(k, carry):
        c = k // CH
        j = k - c * CH
        tile = k // (2 * CH)
        back = 127 - 4 * j - 2 * (c - 2 * tile)
        m = k < kmt
        h = s[0, k]
        un = jnp.where(m, q[0, k] + au, 0.0)
        vn = jnp.where(m, q[1, k] + av, 0.0)
        out[0, k] = un
        out[1, k] = vn
        h5 = (0.5 * DT) * h
        fu, fv = h5 * un, h5 * vn

        def halo(n):
            return roll(col[n, tile], back)

        def row_n(n):
            return rows[4 + n, pl.ds(k, 1), :]

        def row_s(n):
            return rows[n, pl.ds(k, 1), :]

        hal = halo(0)
        e = jnp.where(lane == 127, hal, roll(fu, -1))
        w = jnp.where(lane == 0, hal, roll(fu, 1))
        hn = h - ((e - w) + (from_north(fv, row_n(0)) - from_south(fv, row_s(0))))
        out[2, k] = jnp.where(m, hn, 0.0)
        ke, kw, kn, ks = kd - fu, kd + fu, kd - fv, kd + fv
        mid = h - 4.0 * kd
        for n in range(1, 4):
            x = jnp.where(m, s[n, k], 0.0)
            hal = halo(n)
            e = jnp.where(lane == 127, hal, roll(x * ke, -1))
            w = jnp.where(lane == 0, hal, roll(x * kw, 1))
            r = from_north(x * kn, row_n(n)) + from_south(x * ks, row_s(n))
            out[2 + n, k] = jnp.where(m, (e + w) + (r + x * mid), 0.0)
        return carry

    for i in range(K // LB):
        at = slice(i * LB, (i + 1) * LB)
        lax.fori_loop(i * LB, (i + 1) * LB, body, 0, unroll=UNROLL)
        cp = pltpu.make_async_copy(out.at[:, at], out_hbm.at[:, at], out_sem.at[i])
        cp.start()
        copies.append(cp)
    for cp in copies:
        cp.wait()


def call_b(*operands):
    hbm = pl.BlockSpec(memory_space=pltpu.HBM)
    return pl.pallas_call(
        kernel_b,
        out_shape=(
            jax.ShapeDtypeStruct((6, K, R, C), F32),
            jax.ShapeDtypeStruct((3, R, C), F32),
        ),
        in_specs=[pl.BlockSpec(memory_space=pltpu.VMEM)] * len(operands),
        out_specs=(hbm, hbm),
        scratch_shapes=[
            pltpu.VMEM((6, K, R, C), F32),
            pltpu.SemaphoreType.DMA((K // LB + 1,)),
        ],
        compiler_params=pltpu.CompilerParams(vmem_limit_bytes=24 * 2**20),
        name="transport",
    )(*operands)


def per_device(layers, kmt, barotropic):
    return call_b(*call_a(layers, kmt, barotropic))


def solution(mesh):
    return jax.shard_map(
        per_device,
        mesh=mesh,
        in_specs=(P(None, None, "lat", "lon"), P("lat", "lon"), P(None, "lat", "lon")),
        out_specs=(P(None, None, "lat", "lon"), P(None, "lat", "lon")),
        check_vma=False,
    )
```

```python
import jax
import jax.numpy as jnp
from jax import lax
from jax.experimental import pallas as pl
from jax.experimental.pallas import tpu as pltpu
from jax.sharding import PartitionSpec as P

K = 100
NSUB = 16
R = 32
C = 128
CH = 25
UNROLL = 5
NY = 256

DT = 0.1
TAU = 0.6
NU = 0.01
KAPPA = 0.1
GRAV = 0.1
THERMAL = 1.0
HALINE = 0.8
ROT = 0.5

PSCALE = 1.0 / (4.0 * NU)

F32 = jnp.float32
BF16 = jnp.bfloat16
MESH = pl.DeviceIdType.MESH


def lanes(shape=(1, C)):
    return lax.broadcasted_iota(jnp.int32, shape, 1)


def sublanes(shape):
    return lax.broadcasted_iota(jnp.int32, shape, 0)


def split(x, parts):
    out = []
    for _ in range(parts):
        out.append(x.astype(BF16))
        x = x - out[-1].astype(F32)
    return jnp.concatenate(out, axis=1)


def roll(x, s):
    if isinstance(s, int):
        s %= C
        if s == 0:
            return x
    return pltpu.roll(x, s, axis=1)


def kernel_a(
    layers, kmt_hbm, baro_hbm,
    q, s, kmt_ref, a2d_out, baro_out, col_out, row_out,
    uv, p, baro_ref, cuv, cs, q_edge,
    m_uv, r_uv, m_p, r_p, m_s, r_s, m_q, r_q,
    d4, corr, shift,
    b1, m1, r1, b2, m2, r2, a0v, r_a0v, r_rows, r_qrows,
    eta, ua, vv, dvv, da, dv, c2, c2a, cfa, cfv, sa, sv,
    load_sem, send_sem, recv_sem,
):
    lon = lax.axis_index("lon")
    lat = lax.axis_index("lat")
    nlon = lax.axis_size("lon")
    nlat = lax.axis_size("lat")
    east = lax.rem(lon + 1, nlon)
    west = lax.rem(lon + nlon - 1, nlon)
    north = lax.rem(lat + 1, nlat)
    south = lax.rem(lat + nlat - 1, nlat)
    x_of = {-1: west, 0: lon, 1: east}
    y_of = {-1: south, 0: lat, 1: north}

    loads = {}
    n_load = 0
    for name, src, dst in (("kmt", kmt_hbm, kmt_ref), ("baro", baro_hbm, baro_ref)):
        cp = pltpu.make_async_copy(src, dst, load_sem.at[n_load])
        cp.start()
        loads[name] = cp
        n_load += 1
    half = [slice(0, K // 2), slice(K // 2, K)]
    for i in range(2):
        cp = pltpu.make_async_copy(layers.at[0:2, half[i]], uv.at[0:2, half[i], 8:40, :], load_sem.at[n_load])
        cp.start()
        loads["uv", i] = cp
        n_load += 1
        for c in (2 * i, 2 * i + 1):
            cp = pltpu.make_async_copy(
                layers.at[2:5, c * CH:(c + 1) * CH], s.at[0:3, c * CH:(c + 1) * CH], load_sem.at[n_load])
            cp.start()
            loads["s", c] = cp
            n_load += 1
    cp = pltpu.make_async_copy(layers.at[5], s.at[3], load_sem.at[n_load])
    cp.start()
    loads["age"] = cp

    barrier = pltpu.get_barrier_semaphore()
    around = [(dx, dy) for dx in (-1, 0, 1) for dy in (-1, 0, 1) if (dx, dy) != (0, 0)]
    for dx, dy in around:
        pl.semaphore_signal(barrier, inc=1, device_id=(x_of[dx], y_of[dy]), device_id_type=MESH)

    copies = {}

    def send(name, src, dst, dx, dy):
        at = len(copies)
        cp = pltpu.make_async_remote_copy(
            src_ref=src, dst_ref=dst, send_sem=send_sem.at[at], recv_sem=recv_sem.at[at],
            device_id=(x_of[dx], y_of[dy]), device_id_type=MESH)
        cp.start()
        copies[name] = cp

    lane = lanes()
    quad = lane >> 2
    in_quad = lane & 3
    loads["kmt"].wait()
    loads["baro"].wait()
    kmt = kmt_ref[...]
    cmask = (kmt > 0).astype(F32)

    for c in range(4):
        q_edge[c] = jnp.zeros((R, C), F32)

    b1[1, 40:72, :] = baro_ref[1] * cmask
    b1[2, 40:72, :] = baro_ref[2] * cmask
    b1[3, 40:72, :] = kmt.astype(F32)

    def pack(fields):
        def body(j, accs):
            sel = quad == j
            xs = []
            for load, masked, _, _, c in fields:
                k = c * CH + j
                x = load(k)
                xs.append(jnp.where(k < kmt, x, 0.0) if masked else x)
            out = tuple(jnp.where(sel, roll(x, 4 * j + 2), acc) for x, acc in zip(xs, accs))
            for x, (_, _, store, _, c) in zip(xs, fields):
                if store is not None:
                    uv[store, c * CH + j, 8:40, :] = x
            return out

        accs = lax.fori_loop(0, CH, body, (jnp.zeros((R, C), F32),) * len(fields), unroll=UNROLL)
        for (_, _, _, put, c), acc in zip(fields, accs):
            put(c, acc)

    def put_cuv(f):
        def put(c, x):
            cuv[f, c, 8:40, :] = x
        return put

    def put_cs(f):
        def put(c, x):
            cs[f, c] = x
        return put

    def velocities(i):
        return [(lambda k, f=f: uv[f, k, 8:40, :], True, f, put_cuv(f), c) for f in range(2) for c in (2 * i, 2 * i + 1)]

    def pressures(i):
        return [(lambda k: p[k, 8:40, :], False, None, put_cs(0), c) for c in (2 * i, 2 * i + 1)]

    def scalars(f):
        return [(lambda k: s[f, k], True, None, put_cs(1 + f), c) for c in range(4)]

    def compact(field, lane_from, chunks=(0, 1, 2, 3)):
        out = roll(cs[field, chunks[0]], chunks[0] - lane_from)
        for c in chunks[1:]:
            out = jnp.where(in_quad == c, roll(cs[field, c], c - lane_from), out)
        return out

    def send_velocities(i):
        both = slice(2 * i, 2 * i + 2)
        for c in (2 * i, 2 * i + 1):
            cu, cv = cuv[0, c, 8:40, :], cuv[1, c, 8:40, :]
            m_uv[0, c] = jnp.where(in_quad < 2, cu, roll(cv, 2))
            m_uv[1, c] = jnp.where(in_quad < 2, roll(cu, -2), cv)
        for d, dx in ((0, 1), (1, -1)):
            send(("uv", dx, 1, i), m_uv.at[d, both, 31:32, :], r_uv.at[d, both, 7:8, :], dx, 1)
            send(("uv", dx, -1, i), m_uv.at[d, both, 0:1, :], r_uv.at[d, both, 40:41, :], dx, -1)
            send(("uv", dx, 0, i), m_uv.at[d, both], r_uv.at[d, both, 8:40, :], dx, 0)
        send(("cuv_n", i), cuv.at[:, both, 39:40, :], cuv.at[:, both, 7:8, :], 0, 1)
        send(("cuv_s", i), cuv.at[:, both, 8:9, :], cuv.at[:, both, 40:41, :], 0, -1)

    def send_pressures(i):
        m_p[i, 0] = compact(0, 1, (2 * i, 2 * i + 1))
        m_p[i, 1] = compact(0, 2, (2 * i, 2 * i + 1))
        send(("p_e", i), m_p.at[i, 0], r_p.at[i, 0], 1, 0)
        send(("p_w", i), m_p.at[i, 1], r_p.at[i, 1], -1, 0)
        send(("p_n", i), p.at[half[i], 39, :], p.at[half[i], 7, :], 0, 1)
        send(("p_s", i), p.at[half[i], 8, :], p.at[half[i], 40, :], 0, -1)

    loads["uv", 0].wait()
    pack(velocities(0))

    pl.semaphore_wait(barrier, 8)
    for i in range(2):
        send(("uv_n", i), layers.at[0:2, half[i], 30:32, :], uv.at[:, half[i], 6:8, :], 0, 1)
        send(("uv_s", i), layers.at[0:2, half[i], 0:2, :], uv.at[:, half[i], 40:42, :], 0, -1)
        if i == 0:
            send("b1_n", b1.at[1:4, 40:72, :], b1.at[1:4, 8:40, :], 0, 1)
            send("b1_s", b1.at[1:4, 40:72, :], b1.at[1:4, 72:104, :], 0, -1)
    send_velocities(0)

    zero = jnp.zeros((R, C), F32)
    csum, total = zero, zero
    for c in range(4):
        loads["s", c].wait()

        def body(j, carry, c=c):
            csum, total = carry
            k = c * CH + j
            m = k < kmt
            h = jnp.where(m, s[0, k], 0.0)
            w = ((PSCALE * GRAV * HALINE) * s[2, k] - (PSCALE * GRAV * THERMAL) * s[1, k]) * h
            pk = csum + 0.5 * w
            p[k, 8:40, :] = pk
            return csum + w, total + h

        csum, total = lax.fori_loop(0, CH, body, (csum, total), unroll=UNROLL)
        if c == 1:
            loads["uv", 1].wait()
            pack(pressures(0) + velocities(1))
            send_pressures(0)
            send_velocities(1)

    b1[0, 40:72, :] = total * (1.0 / K)

    def side(fields, eastward):
        out = None
        for n, x in enumerate(fields):
            moved = roll(x, 32 * n + 32) if eastward else roll(x, 32 * n)
            out = moved if out is None else jnp.where(lane < 32 * n, out, moved)
        return out

    def unside(n, d):
        return (roll(d[0], 96 - 32 * n), roll(d[1], -32 * n))

    mine = [b1[n, 40:72, :] for n in range(3)]
    m1[0] = side(mine, True)
    m1[1] = side(mine, False)

    def send_sides(tag, m, r):
        for d, dx in ((0, 1), (1, -1)):
            send((tag, dx, 1), m.at[d], r.at[d, 0:32, :], dx, 1)
            send((tag, dx, -1), m.at[d], r.at[d, 64:96, :], dx, -1)
            send((tag, dx, 0), m.at[d], r.at[d, 32:64, :], dx, 0)

    send("d_n", b1.at[0, 40:72, :], b1.at[0, 8:40, :], 0, 1)
    send("d_s", b1.at[0, 40:72, :], b1.at[0, 72:104, :], 0, -1)
    send_sides("b1", m1, r1)

    def send_scalars(which):
        for f in which:
            m_s[0, f] = compact(1 + f, 1)
            m_s[1, f] = compact(1 + f, 2)

    pack(pressures(1) + scalars(0))
    send_pressures(1)
    pack(scalars(1))
    loads["age"].wait()
    send("s_n", s.at[:, :, 31, :], r_rows.at[0], 0, 1)
    send("s_s", s.at[:, :, 0, :], r_rows.at[1], 0, -1)

    def tiles_of(n, centre, r, at):
        lo, hi = at
        t0 = centre[n, 8 + lo:8 + hi, :]
        from_west, from_east = unside(n, (r[0, lo:hi, :], r[1, lo:hi, :]))
        t1 = jnp.where(lane < 32, from_east, jnp.where(lane >= 96, from_west, 0.0))
        return t0, t1

    def shift_west(t0, t1):
        a, b = roll(t0, 1), roll(t1, 1)
        return jnp.where(lane < 1, b, a), jnp.where(lane < 1, a, b)

    def next_height(lo, both):
        n = 2 if both else 1
        at = pl.ds(lo, 8)
        x = [da[t, at, :] * ua[t, at, :] for t in range(2)]
        r = [roll(x[t], -2) for t in range(2)]
        out = []
        for t in range(n):
            diff = jnp.where(lane < 126, r[t], r[1 - t]) - x[t]
            diff = diff + (dvv[t, pl.ds(lo + 1, 8), :] - dvv[t, pl.ds(lo - 1, 8), :])
            out.append(c2[t, at, :] * diff)
        return out

    def prepare_surface():
        for name in ("d_n", "d_s"):
            copies[name].wait_recv()
        for dx in (1, -1):
            for dy in (0, 1, -1):
                copies["b1", dx, dy].wait_recv()
        for ref in (eta, dvv):
            for t in range(2):
                ref[t, 0:8, :] = jnp.zeros((8, C), F32)
                ref[t, 104:112, :] = jnp.zeros((8, C), F32)
        for blk in range(3):
            at = (32 * blk, 32 * blk + 32)
            here = slice(8 + 32 * blk, 40 + 32 * blk)
            dd = tiles_of(0, b1, r1, at)
            uu = tiles_of(1, b1, r1, at)
            ww = tiles_of(2, b1, r1, at)
            dda = shift_west(*dd)
            uua = shift_west(*uu)
            for t in range(2):
                da[t, here, :] = dda[t]
                ua[t, here, :] = uua[t]
                dv[t, here, :] = dd[t]
                vv[t, here, :] = ww[t]
                dvv[t, here, :] = dd[t] * ww[t]
                c2[t, here, :] = jnp.where(dd[t] > 0.0, 0.5 * TAU, 0.0)
                c2a[t, here, :] = jnp.where(dda[t] > 0.0, 0.5 * TAU, 0.0)

        for i in range(4):
            drop = next_height(40 + 8 * i, False)[0]
            b2[2, 40 + 8 * i:48 + 8 * i, :] = (
                baro_ref[0, 8 * i:8 * i + 8, :] * cmask[8 * i:8 * i + 8] - drop)

    def correct(i):
        for name in ("cuv_n", "cuv_s", "p_e", "p_w", "uv_n", "uv_s", "p_n", "p_s"):
            copies[name, i].wait_recv()
        for dx in (1, -1):
            for dy in (0, 1, -1):
                copies["uv", dx, dy, i].wait_recv()
        p_w, p_e = r_p[i, 0], r_p[i, 1]
        for c in (2 * i, 2 * i + 1):
            w, e = r_uv[0, c], r_uv[1, c]
            d4[0, c] = jnp.where(in_quad < 2, w, roll(e, 2)) - cuv[0, c]
            d4[1, c] = jnp.where(in_quad < 2, roll(w, -2), e) - cuv[1, c]
        for c in (2 * i, 2 * i + 1):
            for f in range(2):
                x = d4[f, c, 8:40, :]
                g = 2.0 * (d4[f, c, 9:41, :] + d4[f, c, 7:39, :]) - 8.0 * x
                out = jnp.where(in_quad < 2, roll(x, -2), roll(x, 2))
                out = out + jnp.where(in_quad == 1, roll(g, -1), jnp.where(in_quad == 2, roll(g, 1), 0.0))
                out = 0.5 * out
                if f == 0:
                    own = cs[0, c]
                    at_127 = roll(p_e, 1 - c) - roll(own, -1)
                    at_0 = roll(own, 1) - roll(p_w, 2 - c)
                    out = out + jnp.where(in_quad == 1, at_127, jnp.where(in_quad == 2, at_0, 0.0))
                corr[f, c] = split(out, 3)

    for name in ("b1_n", "b1_s"):
        copies[name].wait_recv()

    row = sublanes((R, C)) + lat * R
    cor = DT * ROT * (2.0 * (row.astype(F32) + 0.5) / NY - 1.0)

    rim = {at: b1[3, at + 32:at + 40, :] for at in (6, 7, 33, 34)}

    def shifted(f, k, by, seen):
        lo = 8 + by
        x = uv[f, k, lo:lo + R, :]
        at = lo if by < 0 else lo + 24
        if by < 0:
            return jnp.concatenate([jnp.where(seen[at], x[0:8], 0.0), x[8:]], axis=0)
        return jnp.concatenate([x[:24], jnp.where(seen[at], x[24:], 0.0)], axis=0)

    def stencil(f, k, seen):
        x = uv[f, k, 8:40, :]
        one = shifted(f, k, 1, seen) + shifted(f, k, -1, seen)
        two = shifted(f, k, 2, seen) + shifted(f, k, -2, seen)
        return x, one - 4.0 * x, 0.5 * two + (10.0 * x - 4.0 * one)

    i = lax.broadcasted_iota(jnp.int32, (5 * C, C), 0)
    to = lax.broadcasted_iota(jnp.int32, (5 * C, C), 1)
    apart = (to - i) & (C - 1)
    far = jnp.where((apart == 2) | (apart == C - 2), 0.5, 0.0)
    edge = jnp.where(to == ((126 + (i & 3)) & (C - 1)), 1.0, 0.0)
    shift[...] = jnp.where(i < 2 * C, far, edge).astype(BF16)
    quad3 = lax.broadcasted_iota(jnp.int32, (1, 3 * C), 1) % C >> 2

    def level(k, j, extra, sums, acc):
        sgu, sgv, squ, sqv = sums
        m = k < kmt
        kf = k.astype(F32)
        seen = {at: kf < x for at, x in rim.items()}
        u0, unear, gu = stencil(0, k, seen)
        v0, vnear, gv = stencil(1, k, seen)
        pk = p[k, 8:40, :]
        ue = roll(unear + pk, -1)
        uw = roll(unear - pk, 1)
        ve, vw = roll(vnear, -1), roll(vnear, 1)
        gv = gv + (p[k, 9:41, :] - p[k, 7:39, :])
        gu = (gu + extra[0]) + (ue + uw)
        gv = (gv + extra[1]) + (ve + vw)
        gu = jnp.where(m, cor * v0 - (2.0 * DT * NU) * gu, 0.0)
        gv = jnp.where(m, -cor * u0 - (2.0 * DT * NU) * gv, 0.0)
        qu = u0 + gu
        qv = v0 + gv
        q[0, k] = qu
        q[1, k] = qv
        h = s[0, k]
        acc = jnp.where(quad == j, roll(qu, 4 * j + 2), acc)
        return (sgu + gu * h, sgv + gv * h, squ + qu * h, sqv + qv * h), acc

    sums = (zero,) * 4
    for i in range(2):
        correct(i)

        def body(n, sums):
            c = n // 5
            acc = zero
            j0 = 5 * (n - 5 * c)
            left = []
            for l in range(5):
                on = (quad3 == j0 + l).astype(F32).astype(BF16)
                for f in range(2):
                    left.append(jnp.concatenate([split(uv[f, 5 * n + l, 8:40, :], 2), corr[f, c] * on], axis=1))
            moved = jnp.dot(jnp.concatenate(left, axis=0), shift[...], preferred_element_type=F32)
            for l in range(5):
                extra = [moved[R * (2 * l + f):R * (2 * l + f + 1)] for f in range(2)]
                sums, acc = level(5 * n + l, j0 + l, extra, sums, acc)
            q_edge[c] = q_edge[c] + acc
            return sums

        sums = lax.fori_loop(10 * i, 10 * i + 10, body, sums)
        if i == 0:
            prepare_surface()
    for c in range(4):
        cs[0, c] = q_edge[c]
    sgu, sgv, squ, sqv = sums

    bound = jnp.maximum(total, 1.0)
    fu, fv = (1.0 / DT) * sgu / bound, (1.0 / DT) * sgv / bound
    a0u = -DT * fu - (squ - DT * fu * total) / bound
    a0v[...] = -DT * fv - (sqv - DT * fv * total) / bound
    b2[0, 40:72, :] = fu
    b2[1, 40:72, :] = fv
    mine = [fu, fv, b2[2, 40:72, :], a0u]
    m2[0] = side(mine, True)
    m2[1] = side(mine, False)
    send_sides("b2", m2, r2)
    send("b2_n", b2.at[:, 40:72, :], b2.at[:, 8:40, :], 0, 1)
    send("b2_s", b2.at[:, 40:72, :], b2.at[:, 72:104, :], 0, -1)
    send("a_n", a0v.at[24:32, :], r_a0v.at[0], 0, 1)
    send("a_s", a0v.at[0:8, :], r_a0v.at[1], 0, -1)
    m_q[0] = compact(0, 1)
    m_q[1] = compact(0, 2)
    send("q_e", m_q.at[0], r_q.at[0], 1, 0)
    send("q_w", m_q.at[1], r_q.at[1], -1, 0)
    send("q_n", q.at[1, :, 31, :], r_qrows.at[0], 0, 1)
    send("q_s", q.at[1, :, 0, :], r_qrows.at[1], 0, -1)
    pack(scalars(2) + scalars(3))
    send_scalars(range(4))
    send("s_e", m_s.at[0], r_s.at[0], 1, 0)
    send("s_w", m_s.at[1], r_s.at[1], -1, 0)

    for name in ("b2_n", "b2_s"):
        copies[name].wait_recv()
    for dx in (1, -1):
        for dy in (0, 1, -1):
            copies["b2", dx, dy].wait_recv()
    for blk in range(3):
        at = (32 * blk, 32 * blk + 32)
        here = slice(8 + 32 * blk, 40 + 32 * blk)
        ffu = shift_west(*tiles_of(0, b2, r2, at))
        ffv = tiles_of(1, b2, r2, at)
        ee = tiles_of(2, b2, r2, at)
        for t in range(2):
            eta[t, here, :] = ee[t]
            cfa[t, here, :] = 2.0 * c2a[t, here, :] * ffu[t]
            cfv[t, here, :] = 2.0 * c2[t, here, :] * ffv[t]

    sa[...] = jnp.zeros((2, R, C), F32)
    sv[...] = jnp.zeros((48, C), F32)

    def flows(first, count):
        for i in range(count):
            lo = 8 + 8 * (first + i)
            at = slice(lo, lo + 8)
            e = [eta[t, at, :] for t in range(2)]
            r = [roll(e[t], 2) for t in range(2)]
            for t in range(2):
                diff = e[t] - jnp.where(lane < 2, r[1 - t], r[t])
                new_u = ua[t, at, :] + (cfa[t, at, :] - c2a[t, at, :] * diff)
                ua[t, at, :] = new_u
                diff = eta[t, lo + 1:lo + 9, :] - eta[t, lo - 1:lo + 7, :]
                new_v = vv[t, at, :] + (cfv[t, at, :] - c2[t, at, :] * diff)
                vv[t, at, :] = new_v
                dvv[t, at, :] = dv[t, at, :] * new_v
                if 40 <= lo < 72:
                    sa[t, lo - 40:lo - 32, :] += new_u
                if t == 0 and 32 <= lo < 80:
                    sv[lo - 32:lo - 24, :] += new_v

    def heights(first, count):
        for i in range(count):
            lo = 8 + 8 * (first + i)
            drop = next_height(lo, True)
            for t in range(2):
                eta[t, lo:lo + 8, :] = eta[t, lo:lo + 8, :] - drop[t]

    flows(0, 12)
    for group in range(4):
        first, count = group, 12 - 2 * group

        def body(n, carry, first=first, count=count):
            heights(first, count)
            flows(first, count)
            return carry

        lax.fori_loop(0, 3 if group == 0 else 4, body, 0)

    sa0, sa1 = sa[0], sa[1]
    su = jnp.where(lane < 127, roll(sa0, -1), roll(sa1, -1))
    a2d_out[0] = a0u + su * (1.0 / NSUB)
    a2d_out[1] = a0v[...] + sv[8:40, :] * (1.0 / NSUB)
    baro_out[0] = eta[0, 40:72, :]
    baro_out[1] = jnp.where(lane < 127, roll(ua[0, 40:72, :], -1), roll(ua[1, 40:72, :], -1))
    baro_out[2] = vv[0, 40:72, :]

    for name in ("s_e", "s_w", "q_e", "q_w"):
        copies[name].wait_recv()
    a_w = r2[0, 32:64, 127:128] + sa0[:, 0:1] * (1.0 / NSUB)
    a_e = r2[1, 32:64, 96:97] + sa1[:, 1:2] * (1.0 / NSUB)
    halves = []
    for d, a, sign in ((0, a_w, 1.0), (1, a_e, -1.0)):
        flux = (0.5 * DT) * r_s[d, 0] * (r_q[d] + a)
        vals = [flux]
        for n in range(1, 4):
            vals.append(r_s[d, n] * ((DT * KAPPA) + sign * flux))
        halves.append(vals)
    for n in range(4):
        w, e = halves[0][n], halves[1][n]
        col_out[n, 0] = jnp.where(
            in_quad == 0, e, jnp.where(in_quad == 1, roll(w, 1), jnp.where(in_quad == 2, roll(e, 1), roll(w, 2))))
        col_out[n, 1] = jnp.where(
            in_quad == 0, roll(e, -2), jnp.where(in_quad == 1, roll(w, -1), jnp.where(in_quad == 2, roll(e, -1), w)))

    for name in ("s_n", "s_s", "q_n", "q_s", "a_n", "a_s"):
        copies[name].wait_recv()
    level = sublanes((K, C)).astype(F32)
    for d, kmt_row, a_row, sign in (
        (0, b1[3, 39:40, :], r_a0v[0, 7:8, :] + sv[7:8, :] * (1.0 / NSUB), 1.0),
        (1, b1[3, 72:73, :], r_a0v[1, 0:1, :] + sv[40:41, :] * (1.0 / NSUB), -1.0),
    ):
        m = level < kmt_row
        flux = jnp.where(m, (0.5 * DT) * r_rows[d, 0] * (r_qrows[d] + a_row), 0.0)
        row_out[4 * d] = flux
        for n in range(1, 4):
            row_out[4 * d + n] = jnp.where(m, r_rows[d, n], 0.0) * ((DT * KAPPA) + sign * flux)

    for cp in copies.values():
        cp.wait_send()


N_COPIES = 2 * (2 + 8 + 4) + 10 + 4 + 14


def call_a(layers, kmt, baro):
    v = lambda *shape: pltpu.VMEM(shape, F32)
    surface = [v(2, 112, C) for _ in range(10)]
    vmem = pl.BlockSpec(memory_space=pltpu.VMEM)
    shape = lambda *dims: jax.ShapeDtypeStruct(dims, F32)
    return pl.pallas_call(
        kernel_a,
        out_shape=(
            shape(2, K, R, C), shape(4, K, R, C), jax.ShapeDtypeStruct((R, C), jnp.int32),
            shape(2, R, C), shape(3, R, C), shape(4, 2, R, C), shape(8, K, C),
        ),
        in_specs=[pl.BlockSpec(memory_space=pltpu.HBM)] * 3,
        out_specs=(vmem,) * 7,
        scratch_shapes=[
            v(2, K, 48, C), v(K, 48, C), v(3, R, C), v(2, 4, 48, C), v(5, 4, R, C), v(4, R, C),
            v(2, 4, R, C), v(2, 4, 48, C), v(2, 2, R, C), v(2, 2, R, C), v(2, 4, R, C), v(2, 4, R, C), v(2, R, C), v(2, R, C),
            v(2, 4, 48, C), pltpu.VMEM((2, 4, R, 3 * C), BF16), pltpu.VMEM((5 * C, C), BF16),
            v(4, 112, C), v(2, R, C), v(2, 96, C), v(3, 112, C), v(2, R, C), v(2, 96, C),
            v(R, C), v(2, 8, C), v(2, 4, K, C), v(2, K, C),
            *surface, v(2, R, C), v(48, C),
            pltpu.SemaphoreType.DMA((9,)),
            pltpu.SemaphoreType.DMA((N_COPIES,)),
            pltpu.SemaphoreType.DMA((N_COPIES,)),
        ],
        compiler_params=pltpu.CompilerParams(
            collective_id=0, has_side_effects=True, vmem_limit_bytes=24 * 2**20),
        name="tendencies_and_surface",
    )(*(pltpu.with_memory_space_constraint(x, pltpu.HBM) for x in (layers, kmt, baro)))


LB = 10


def kernel_b(q, s, kmt_ref, a2d, baro, col, rows, out_hbm, baro_hbm, out, out_sem):
    lane = lanes()
    sub = sublanes((8, C))
    kmt = kmt_ref[...]
    au, av = a2d[0], a2d[1]
    kd = DT * KAPPA

    copies = [pltpu.make_async_copy(baro, baro_hbm, out_sem.at[K // LB])]
    copies[0].start()

    def tiles(x):
        return [x[8 * i:8 * i + 8] for i in range(4)]

    def from_north(x, halo):
        r = [pltpu.roll(t, 7, axis=0) for t in tiles(x)] + [jnp.broadcast_to(halo, (8, C))]
        return jnp.concatenate([jnp.where(sub == 7, r[i + 1], r[i]) for i in range(4)], axis=0)

    def from_south(x, halo):
        r = [jnp.broadcast_to(halo, (8, C))] + [pltpu.roll(t, 1, axis=0) for t in tiles(x)]
        return jnp.concatenate([jnp.where(sub == 0, r[i], r[i + 1]) for i in range(4)], axis=0)

    def level(k):
        c = k // CH
        j = k - c * CH
        tile = k // (2 * CH)
        back = 127 - 4 * j - 2 * (c - 2 * tile)
        m = k < kmt
        h = s[0, k]
        un = jnp.where(m, q[0, k] + au, 0.0)
        vn = jnp.where(m, q[1, k] + av, 0.0)
        out[0, k] = un
        out[1, k] = vn
        h5 = (0.5 * DT) * h
        fu, fv = h5 * un, h5 * vn

        def halo(n):
            return roll(col[n, tile], back)

        def row_n(n):
            return rows[4 + n, k:k + 1, :]

        def row_s(n):
            return rows[n, k:k + 1, :]

        hal = halo(0)
        e = jnp.where(lane == 127, hal, roll(fu, -1))
        w = jnp.where(lane == 0, hal, roll(fu, 1))
        hn = h - ((e - w) + (from_north(fv, row_n(0)) - from_south(fv, row_s(0))))
        out[2, k] = jnp.where(m, hn, 0.0)
        ke, kw, kn, ks = kd - fu, kd + fu, kd - fv, kd + fv
        mid = h - 4.0 * kd
        for n in range(1, 4):
            x = jnp.where(m, s[n, k], 0.0)
            hal = halo(n)
            e = jnp.where(lane == 127, hal, roll(x * ke, -1))
            w = jnp.where(lane == 0, hal, roll(x * kw, 1))
            r = from_north(x * kn, row_n(n)) + from_south(x * ks, row_s(n))
            out[2 + n, k] = jnp.where(m, (e + w) + (r + x * mid), 0.0)

    def put(i):
        at = slice(i * LB, (i + 1) * LB)
        return pltpu.make_async_copy(out.at[:, at], out_hbm.at[:, at], out_sem.at[i])

    for i in range(K // LB):
        for k in range(i * LB, (i + 1) * LB):
            level(k)
        put(i).start()
    for i in range(K // LB):
        put(i).wait()
    copies[0].wait()


def call_b(*operands):
    hbm = pl.BlockSpec(memory_space=pltpu.HBM)
    return pl.pallas_call(
        kernel_b,
        out_shape=(
            jax.ShapeDtypeStruct((6, K, R, C), F32),
            jax.ShapeDtypeStruct((3, R, C), F32),
        ),
        in_specs=[pl.BlockSpec(memory_space=pltpu.VMEM)] * len(operands),
        out_specs=(hbm, hbm),
        scratch_shapes=[
            pltpu.VMEM((6, K, R, C), F32),
            pltpu.SemaphoreType.DMA((K // LB + 1,)),
        ],
        compiler_params=pltpu.CompilerParams(vmem_limit_bytes=24 * 2**20),
        name="transport",
    )(*operands)


def per_device(layers, kmt, barotropic):
    return call_b(*call_a(layers, kmt, barotropic))


def solution(mesh):
    return jax.shard_map(
        per_device,
        mesh=mesh,
        in_specs=(P(None, None, "lat", "lon"), P("lat", "lon"), P(None, "lat", "lon")),
        out_specs=(P(None, None, "lat", "lon"), P(None, "lat", "lon")),
        check_vma=False,
    )
```

```python
import jax
import jax.numpy as jnp
from jax import lax
from jax.experimental import pallas as pl
from jax.experimental.pallas import tpu as pltpu
from jax.sharding import PartitionSpec as P

K = 100
NSUB = 16
R = 32
C = 128
CH = 25
UNROLL = 5
NY = 256

DT = 0.1
TAU = 0.6
NU = 0.01
KAPPA = 0.1
GRAV = 0.1
THERMAL = 1.0
HALINE = 0.8
ROT = 0.5

PSCALE = 1.0 / (4.0 * NU)

F32 = jnp.float32
BF16 = jnp.bfloat16
MESH = pl.DeviceIdType.MESH


def lanes(shape=(1, C)):
    return lax.broadcasted_iota(jnp.int32, shape, 1)


def sublanes(shape):
    return lax.broadcasted_iota(jnp.int32, shape, 0)


def split(x, parts):
    out = []
    for _ in range(parts):
        out.append(x.astype(BF16))
        x = x - out[-1].astype(F32)
    return jnp.concatenate(out, axis=1)


def roll(x, s):
    if isinstance(s, int):
        s %= C
        if s == 0:
            return x
    return pltpu.roll(x, s, axis=1)


def kernel_a(
    layers, kmt_hbm, baro_hbm,
    q, s, kmt_ref, a2d_out, baro_out, col_out, row_out,
    uv, p, baro_ref, cuv, cs,
    m_uv, r_uv, m_p, r_p, m_s, r_s, m_q, r_q,
    d4, corr, shift,
    b1, m1, r1, b2, m2, r2, a0v, r_a0v, r_rows, r_qrows,
    eta, ua, vv, dvv, da, dv, c2, c2a, cfa, cfv, sa, sv,
    load_sem, send_sem, recv_sem,
):
    lon = lax.axis_index("lon")
    lat = lax.axis_index("lat")
    nlon = lax.axis_size("lon")
    nlat = lax.axis_size("lat")
    east = lax.rem(lon + 1, nlon)
    west = lax.rem(lon + nlon - 1, nlon)
    north = lax.rem(lat + 1, nlat)
    south = lax.rem(lat + nlat - 1, nlat)
    x_of = {-1: west, 0: lon, 1: east}
    y_of = {-1: south, 0: lat, 1: north}

    loads = {}
    n_load = 0
    for name, src, dst in (("kmt", kmt_hbm, kmt_ref), ("baro", baro_hbm, baro_ref)):
        cp = pltpu.make_async_copy(src, dst, load_sem.at[n_load])
        cp.start()
        loads[name] = cp
        n_load += 1
    half = [slice(0, K // 2), slice(K // 2, K)]
    for i in range(2):
        cp = pltpu.make_async_copy(layers.at[0:2, half[i]], uv.at[0:2, half[i], 8:40, :], load_sem.at[n_load])
        cp.start()
        loads["uv", i] = cp
        n_load += 1
        for c in (2 * i, 2 * i + 1):
            cp = pltpu.make_async_copy(
                layers.at[2:5, c * CH:(c + 1) * CH], s.at[0:3, c * CH:(c + 1) * CH], load_sem.at[n_load])
            cp.start()
            loads["s", c] = cp
            n_load += 1
    cp = pltpu.make_async_copy(layers.at[5], s.at[3], load_sem.at[n_load])
    cp.start()
    loads["age"] = cp

    barrier = pltpu.get_barrier_semaphore()
    around = [(dx, dy) for dx in (-1, 0, 1) for dy in (-1, 0, 1) if (dx, dy) != (0, 0)]
    for dx, dy in around:
        pl.semaphore_signal(barrier, inc=1, device_id=(x_of[dx], y_of[dy]), device_id_type=MESH)

    copies = {}

    def send(name, src, dst, dx, dy):
        at = len(copies)
        cp = pltpu.make_async_remote_copy(
            src_ref=src, dst_ref=dst, send_sem=send_sem.at[at], recv_sem=recv_sem.at[at],
            device_id=(x_of[dx], y_of[dy]), device_id_type=MESH)
        cp.start()
        copies[name] = cp

    lane = lanes()
    quad = lane >> 2
    in_quad = lane & 3
    loads["kmt"].wait()
    loads["baro"].wait()
    kmt = kmt_ref[...]
    cmask = (kmt > 0).astype(F32)

    b1[1, 40:72, :] = baro_ref[1] * cmask
    b1[2, 40:72, :] = baro_ref[2] * cmask
    b1[3, 40:72, :] = kmt.astype(F32)

    def pack(fields):
        def body(j, accs):
            sel = quad == j
            xs = []
            for load, masked, _, _, c in fields:
                k = c * CH + j
                x = load(k)
                xs.append(jnp.where(k < kmt, x, 0.0) if masked else x)
            out = tuple(jnp.where(sel, roll(x, 4 * j + 2), acc) for x, acc in zip(xs, accs))
            for x, (_, _, store, _, c) in zip(xs, fields):
                if store is not None:
                    uv[store, c * CH + j, 8:40, :] = x
            return out

        accs = lax.fori_loop(0, CH, body, (jnp.zeros((R, C), F32),) * len(fields), unroll=UNROLL)
        for (_, _, _, put, c), acc in zip(fields, accs):
            put(c, acc)

    def put_cuv(f):
        def put(c, x):
            cuv[f, c, 8:40, :] = x
        return put

    def put_cs(f):
        def put(c, x):
            cs[f, c] = x
        return put

    def velocities(i):
        return [(lambda k, f=f: uv[f, k, 8:40, :], True, f, put_cuv(f), c) for f in range(2) for c in (2 * i, 2 * i + 1)]

    def pressures(i):
        return [(lambda k: p[k, 8:40, :], False, None, put_cs(0), c) for c in (2 * i, 2 * i + 1)]

    def scalars(f):
        return [(lambda k: s[f, k], True, None, put_cs(1 + f), c) for c in range(4)]

    def compact(field, lane_from, chunks=(0, 1, 2, 3)):
        out = roll(cs[field, chunks[0]], chunks[0] - lane_from)
        for c in chunks[1:]:
            out = jnp.where(in_quad == c, roll(cs[field, c], c - lane_from), out)
        return out

    def send_velocities(i):
        both = slice(2 * i, 2 * i + 2)
        for c in (2 * i, 2 * i + 1):
            cu, cv = cuv[0, c, 8:40, :], cuv[1, c, 8:40, :]
            m_uv[0, c] = jnp.where(in_quad < 2, cu, roll(cv, 2))
            m_uv[1, c] = jnp.where(in_quad < 2, roll(cu, -2), cv)
        for d, dx in ((0, 1), (1, -1)):
            send(("uv", dx, 1, i), m_uv.at[d, both, 31:32, :], r_uv.at[d, both, 7:8, :], dx, 1)
            send(("uv", dx, -1, i), m_uv.at[d, both, 0:1, :], r_uv.at[d, both, 40:41, :], dx, -1)
            send(("uv", dx, 0, i), m_uv.at[d, both], r_uv.at[d, both, 8:40, :], dx, 0)
        send(("cuv_n", i), cuv.at[:, both, 39:40, :], cuv.at[:, both, 7:8, :], 0, 1)
        send(("cuv_s", i), cuv.at[:, both, 8:9, :], cuv.at[:, both, 40:41, :], 0, -1)

    def send_pressures(i):
        m_p[i, 0] = compact(0, 1, (2 * i, 2 * i + 1))
        m_p[i, 1] = compact(0, 2, (2 * i, 2 * i + 1))
        send(("p_e", i), m_p.at[i, 0], r_p.at[i, 0], 1, 0)
        send(("p_w", i), m_p.at[i, 1], r_p.at[i, 1], -1, 0)
        send(("p_n", i), p.at[half[i], 39, :], p.at[half[i], 7, :], 0, 1)
        send(("p_s", i), p.at[half[i], 8, :], p.at[half[i], 40, :], 0, -1)

    loads["uv", 0].wait()
    pack(velocities(0))

    pl.semaphore_wait(barrier, 8)
    for i in range(2):
        send(("uv_n", i), layers.at[0:2, half[i], 30:32, :], uv.at[:, half[i], 6:8, :], 0, 1)
        send(("uv_s", i), layers.at[0:2, half[i], 0:2, :], uv.at[:, half[i], 40:42, :], 0, -1)
        if i == 0:
            send("b1_n", b1.at[1:4, 40:72, :], b1.at[1:4, 8:40, :], 0, 1)
            send("b1_s", b1.at[1:4, 40:72, :], b1.at[1:4, 72:104, :], 0, -1)
    send_velocities(0)

    zero = jnp.zeros((R, C), F32)
    csum, total = zero, zero
    for c in range(4):
        loads["s", c].wait()

        def body(j, carry, c=c):
            csum, total = carry
            k = c * CH + j
            m = k < kmt
            h = jnp.where(m, s[0, k], 0.0)
            w = ((PSCALE * GRAV * HALINE) * s[2, k] - (PSCALE * GRAV * THERMAL) * s[1, k]) * h
            pk = csum + 0.5 * w
            p[k, 8:40, :] = pk
            return csum + w, total + h

        csum, total = lax.fori_loop(0, CH, body, (csum, total), unroll=UNROLL)
        if c == 1:
            loads["uv", 1].wait()
            pack(pressures(0) + velocities(1))
            send_pressures(0)
            send_velocities(1)

    b1[0, 40:72, :] = total * (1.0 / K)

    def side(fields, eastward):
        out = None
        for n, x in enumerate(fields):
            moved = roll(x, 32 * n + 32) if eastward else roll(x, 32 * n)
            out = moved if out is None else jnp.where(lane < 32 * n, out, moved)
        return out

    def unside(n, d):
        return (roll(d[0], 96 - 32 * n), roll(d[1], -32 * n))

    mine = [b1[n, 40:72, :] for n in range(3)]
    m1[0] = side(mine, True)
    m1[1] = side(mine, False)

    def send_sides(tag, m, r):
        for d, dx in ((0, 1), (1, -1)):
            send((tag, dx, 1), m.at[d], r.at[d, 0:32, :], dx, 1)
            send((tag, dx, -1), m.at[d], r.at[d, 64:96, :], dx, -1)
            send((tag, dx, 0), m.at[d], r.at[d, 32:64, :], dx, 0)

    send("d_n", b1.at[0, 40:72, :], b1.at[0, 8:40, :], 0, 1)
    send("d_s", b1.at[0, 40:72, :], b1.at[0, 72:104, :], 0, -1)
    send_sides("b1", m1, r1)

    def send_scalars(which):
        for f in which:
            m_s[0, f] = compact(1 + f, 1)
            m_s[1, f] = compact(1 + f, 2)

    pack(pressures(1) + scalars(0))
    send_pressures(1)
    pack(scalars(1))
    loads["age"].wait()
    send("s_n", s.at[:, :, 31, :], r_rows.at[0], 0, 1)
    send("s_s", s.at[:, :, 0, :], r_rows.at[1], 0, -1)

    def tiles_of(n, centre, r, at):
        lo, hi = at
        t0 = centre[n, 8 + lo:8 + hi, :]
        from_west, from_east = unside(n, (r[0, lo:hi, :], r[1, lo:hi, :]))
        t1 = jnp.where(lane < 32, from_east, jnp.where(lane >= 96, from_west, 0.0))
        return t0, t1

    def shift_west(t0, t1):
        a, b = roll(t0, 1), roll(t1, 1)
        return jnp.where(lane < 1, b, a), jnp.where(lane < 1, a, b)

    def next_height(lo, both):
        n = 2 if both else 1
        at = pl.ds(lo, 8)
        x = [da[t, at, :] * ua[t, at, :] for t in range(2)]
        r = [roll(x[t], -2) for t in range(2)]
        out = []
        for t in range(n):
            diff = jnp.where(lane < 126, r[t], r[1 - t]) - x[t]
            diff = diff + (dvv[t, pl.ds(lo + 1, 8), :] - dvv[t, pl.ds(lo - 1, 8), :])
            out.append(c2[t, at, :] * diff)
        return out

    def prepare_surface():
        for name in ("d_n", "d_s"):
            copies[name].wait_recv()
        for dx in (1, -1):
            for dy in (0, 1, -1):
                copies["b1", dx, dy].wait_recv()
        for ref in (eta, dvv):
            for t in range(2):
                ref[t, 0:8, :] = jnp.zeros((8, C), F32)
                ref[t, 104:112, :] = jnp.zeros((8, C), F32)
        for blk in range(3):
            at = (32 * blk, 32 * blk + 32)
            here = slice(8 + 32 * blk, 40 + 32 * blk)
            dd = tiles_of(0, b1, r1, at)
            uu = tiles_of(1, b1, r1, at)
            ww = tiles_of(2, b1, r1, at)
            dda = shift_west(*dd)
            uua = shift_west(*uu)
            for t in range(2):
                da[t, here, :] = dda[t]
                ua[t, here, :] = uua[t]
                dv[t, here, :] = dd[t]
                vv[t, here, :] = ww[t]
                dvv[t, here, :] = dd[t] * ww[t]
                c2[t, here, :] = jnp.where(dd[t] > 0.0, 0.5 * TAU, 0.0)
                c2a[t, here, :] = jnp.where(dda[t] > 0.0, 0.5 * TAU, 0.0)

        for i in range(4):
            drop = next_height(40 + 8 * i, False)[0]
            b2[2, 40 + 8 * i:48 + 8 * i, :] = (
                baro_ref[0, 8 * i:8 * i + 8, :] * cmask[8 * i:8 * i + 8] - drop)

    def correct(i):
        for name in ("cuv_n", "cuv_s", "p_e", "p_w", "uv_n", "uv_s", "p_n", "p_s"):
            copies[name, i].wait_recv()
        for dx in (1, -1):
            for dy in (0, 1, -1):
                copies["uv", dx, dy, i].wait_recv()
        p_w, p_e = r_p[i, 0], r_p[i, 1]
        for c in (2 * i, 2 * i + 1):
            w, e = r_uv[0, c], r_uv[1, c]
            d4[0, c] = jnp.where(in_quad < 2, w, roll(e, 2)) - cuv[0, c]
            d4[1, c] = jnp.where(in_quad < 2, roll(w, -2), e) - cuv[1, c]
        for c in (2 * i, 2 * i + 1):
            for f in range(2):
                x = d4[f, c, 8:40, :]
                g = 2.0 * (d4[f, c, 9:41, :] + d4[f, c, 7:39, :]) - 8.0 * x
                out = jnp.where(in_quad < 2, roll(x, -2), roll(x, 2))
                out = out + jnp.where(in_quad == 1, roll(g, -1), jnp.where(in_quad == 2, roll(g, 1), 0.0))
                out = 0.5 * out
                if f == 0:
                    own = cs[0, c]
                    at_127 = roll(p_e, 1 - c) - roll(own, -1)
                    at_0 = roll(own, 1) - roll(p_w, 2 - c)
                    out = out + jnp.where(in_quad == 1, at_127, jnp.where(in_quad == 2, at_0, 0.0))
                corr[f, c] = split(out, 3)

    for name in ("b1_n", "b1_s"):
        copies[name].wait_recv()

    row = sublanes((R, C)) + lat * R
    cor = DT * ROT * (2.0 * (row.astype(F32) + 0.5) / NY - 1.0)

    rim = {at: b1[3, at + 32:at + 40, :] for at in (6, 7, 33, 34)}

    def shifted(f, k, by, seen):
        lo = 8 + by
        x = uv[f, k, lo:lo + R, :]
        at = lo if by < 0 else lo + 24
        if by < 0:
            return jnp.concatenate([jnp.where(seen[at], x[0:8], 0.0), x[8:]], axis=0)
        return jnp.concatenate([x[:24], jnp.where(seen[at], x[24:], 0.0)], axis=0)

    def stencil(f, k, seen):
        x = uv[f, k, 8:40, :]
        one = shifted(f, k, 1, seen) + shifted(f, k, -1, seen)
        two = shifted(f, k, 2, seen) + shifted(f, k, -2, seen)
        return x, one - 4.0 * x, 0.5 * two + (10.0 * x - 4.0 * one)

    i = lax.broadcasted_iota(jnp.int32, (5 * C, C), 0)
    to = lax.broadcasted_iota(jnp.int32, (5 * C, C), 1)
    apart = (to - i) & (C - 1)
    far = jnp.where((apart == 2) | (apart == C - 2), 0.5, 0.0)
    edge = jnp.where(to == ((126 + (i & 3)) & (C - 1)), 1.0, 0.0)
    shift[...] = jnp.where(i < 2 * C, far, edge).astype(BF16)
    quad3 = lax.broadcasted_iota(jnp.int32, (1, 3 * C), 1) % C >> 2

    def level(k, extra, sums):
        sgu, sgv, squ, sqv = sums
        m = k < kmt
        kf = k.astype(F32)
        seen = {at: kf < x for at, x in rim.items()}
        u0, unear, gu = stencil(0, k, seen)
        v0, vnear, gv = stencil(1, k, seen)
        pk = p[k, 8:40, :]
        ue = roll(unear + pk, -1)
        uw = roll(unear - pk, 1)
        ve, vw = roll(vnear, -1), roll(vnear, 1)
        gv = gv + (p[k, 9:41, :] - p[k, 7:39, :])
        gu = (gu + extra[0]) + (ue + uw)
        gv = (gv + extra[1]) + (ve + vw)
        gu = jnp.where(m, cor * v0 - (2.0 * DT * NU) * gu, 0.0)
        gv = jnp.where(m, -cor * u0 - (2.0 * DT * NU) * gv, 0.0)
        qu = u0 + gu
        qv = v0 + gv
        q[0, k] = qu
        q[1, k] = qv
        h = s[0, k]
        return sgu + gu * h, sgv + gv * h, squ + qu * h, sqv + qv * h

    sums = (zero,) * 4
    for i in range(2):
        correct(i)

        def body(n, sums):
            c = n // 5
            j0 = 5 * (n - 5 * c)
            left = [], []
            for l in range(5):
                on = (quad3 == j0 + l).astype(F32).astype(BF16)
                for f in range(2):
                    deep = (5 - f) * C - 2 * C
                    left[f].append(jnp.concatenate([split(uv[f, 5 * n + l, 8:40, :], 2), (corr[f, c] * on)[:, :deep]], axis=1))
            moved = [
                jnp.dot(jnp.concatenate(left[f], axis=0), shift[:(5 - f) * C, :], preferred_element_type=F32)
                for f in range(2)
            ]
            for l in range(5):
                extra = [moved[f][R * l:R * (l + 1)] for f in range(2)]
                sums = level(5 * n + l, extra, sums)
            return sums

        sums = lax.fori_loop(10 * i, 10 * i + 10, body, sums)
        if i == 0:
            prepare_surface()
    sgu, sgv, squ, sqv = sums

    bound = jnp.maximum(total, 1.0)
    fu, fv = (1.0 / DT) * sgu / bound, (1.0 / DT) * sgv / bound
    a0u = -DT * fu - (squ - DT * fu * total) / bound
    a0v[...] = -DT * fv - (sqv - DT * fv * total) / bound
    b2[0, 40:72, :] = fu
    b2[1, 40:72, :] = fv
    mine = [fu, fv, b2[2, 40:72, :], a0u]
    m2[0] = side(mine, True)
    m2[1] = side(mine, False)
    send_sides("b2", m2, r2)
    send("b2_n", b2.at[:, 40:72, :], b2.at[:, 8:40, :], 0, 1)
    send("b2_s", b2.at[:, 40:72, :], b2.at[:, 72:104, :], 0, -1)
    send("a_n", a0v.at[24:32, :], r_a0v.at[0], 0, 1)
    send("a_s", a0v.at[0:8, :], r_a0v.at[1], 0, -1)
    send("q_n", q.at[1, :, 31, :], r_qrows.at[0], 0, 1)
    send("q_s", q.at[1, :, 0, :], r_qrows.at[1], 0, -1)
    pack([(lambda k: q[0, k], False, None, put_cs(0), c) for c in range(4)] + scalars(2))
    m_q[0] = compact(0, 1)
    m_q[1] = compact(0, 2)
    send("q_e", m_q.at[0], r_q.at[0], 1, 0)
    send("q_w", m_q.at[1], r_q.at[1], -1, 0)
    pack(scalars(3))
    send_scalars(range(4))
    send("s_e", m_s.at[0], r_s.at[0], 1, 0)
    send("s_w", m_s.at[1], r_s.at[1], -1, 0)

    for name in ("b2_n", "b2_s"):
        copies[name].wait_recv()
    for dx in (1, -1):
        for dy in (0, 1, -1):
            copies["b2", dx, dy].wait_recv()
    for blk in range(3):
        at = (32 * blk, 32 * blk + 32)
        here = slice(8 + 32 * blk, 40 + 32 * blk)
        ffu = shift_west(*tiles_of(0, b2, r2, at))
        ffv = tiles_of(1, b2, r2, at)
        ee = tiles_of(2, b2, r2, at)
        for t in range(2):
            eta[t, here, :] = ee[t]
            cfa[t, here, :] = 2.0 * c2a[t, here, :] * ffu[t]
            cfv[t, here, :] = 2.0 * c2[t, here, :] * ffv[t]

    sa[...] = jnp.zeros((2, R, C), F32)
    sv[...] = jnp.zeros((48, C), F32)

    def flows(first, count):
        for i in range(count):
            lo = 8 + 8 * (first + i)
            at = slice(lo, lo + 8)
            e = [eta[t, at, :] for t in range(2)]
            r = [roll(e[t], 2) for t in range(2)]
            for t in range(2):
                diff = e[t] - jnp.where(lane < 2, r[1 - t], r[t])
                new_u = ua[t, at, :] + (cfa[t, at, :] - c2a[t, at, :] * diff)
                ua[t, at, :] = new_u
                diff = eta[t, lo + 1:lo + 9, :] - eta[t, lo - 1:lo + 7, :]
                new_v = vv[t, at, :] + (cfv[t, at, :] - c2[t, at, :] * diff)
                vv[t, at, :] = new_v
                dvv[t, at, :] = dv[t, at, :] * new_v
                if 40 <= lo < 72:
                    sa[t, lo - 40:lo - 32, :] += new_u
                if t == 0 and 32 <= lo < 80:
                    sv[lo - 32:lo - 24, :] += new_v

    def heights(first, count):
        for i in range(count):
            lo = 8 + 8 * (first + i)
            drop = next_height(lo, True)
            for t in range(2):
                eta[t, lo:lo + 8, :] = eta[t, lo:lo + 8, :] - drop[t]

    flows(0, 12)
    for group in range(4):
        first, count = group, 12 - 2 * group

        def body(n, carry, first=first, count=count):
            heights(first, count)
            flows(first, count)
            return carry

        lax.fori_loop(0, 3 if group == 0 else 4, body, 0)

    sa0, sa1 = sa[0], sa[1]
    su = jnp.where(lane < 127, roll(sa0, -1), roll(sa1, -1))
    a2d_out[0] = a0u + su * (1.0 / NSUB)
    a2d_out[1] = a0v[...] + sv[8:40, :] * (1.0 / NSUB)
    baro_out[0] = eta[0, 40:72, :]
    baro_out[1] = jnp.where(lane < 127, roll(ua[0, 40:72, :], -1), roll(ua[1, 40:72, :], -1))
    baro_out[2] = vv[0, 40:72, :]

    for name in ("s_e", "s_w", "q_e", "q_w"):
        copies[name].wait_recv()
    a_w = r2[0, 32:64, 127:128] + sa0[:, 0:1] * (1.0 / NSUB)
    a_e = r2[1, 32:64, 96:97] + sa1[:, 1:2] * (1.0 / NSUB)
    halves = []
    for d, a, sign in ((0, a_w, 1.0), (1, a_e, -1.0)):
        flux = (0.5 * DT) * r_s[d, 0] * (r_q[d] + a)
        vals = [flux]
        for n in range(1, 4):
            vals.append(r_s[d, n] * ((DT * KAPPA) + sign * flux))
        halves.append(vals)
    for n in range(4):
        w, e = halves[0][n], halves[1][n]
        col_out[n, 0] = jnp.where(
            in_quad == 0, e, jnp.where(in_quad == 1, roll(w, 1), jnp.where(in_quad == 2, roll(e, 1), roll(w, 2))))
        col_out[n, 1] = jnp.where(
            in_quad == 0, roll(e, -2), jnp.where(in_quad == 1, roll(w, -1), jnp.where(in_quad == 2, roll(e, -1), w)))

    for name in ("s_n", "s_s", "q_n", "q_s", "a_n", "a_s"):
        copies[name].wait_recv()
    level = sublanes((K, C)).astype(F32)
    for d, kmt_row, a_row, sign in (
        (0, b1[3, 39:40, :], r_a0v[0, 7:8, :] + sv[7:8, :] * (1.0 / NSUB), 1.0),
        (1, b1[3, 72:73, :], r_a0v[1, 0:1, :] + sv[40:41, :] * (1.0 / NSUB), -1.0),
    ):
        m = level < kmt_row
        flux = jnp.where(m, (0.5 * DT) * r_rows[d, 0] * (r_qrows[d] + a_row), 0.0)
        row_out[4 * d] = flux
        for n in range(1, 4):
            row_out[4 * d + n] = jnp.where(m, r_rows[d, n], 0.0) * ((DT * KAPPA) + sign * flux)

    for cp in copies.values():
        cp.wait_send()


N_COPIES = 2 * (2 + 8 + 4) + 10 + 4 + 14


def call_a(layers, kmt, baro):
    v = lambda *shape: pltpu.VMEM(shape, F32)
    surface = [v(2, 112, C) for _ in range(10)]
    vmem = pl.BlockSpec(memory_space=pltpu.VMEM)
    shape = lambda *dims: jax.ShapeDtypeStruct(dims, F32)
    return pl.pallas_call(
        kernel_a,
        out_shape=(
            shape(2, K, R, C), shape(4, K, R, C), jax.ShapeDtypeStruct((R, C), jnp.int32),
            shape(2, R, C), shape(3, R, C), shape(4, 2, R, C), shape(8, K, C),
        ),
        in_specs=[pl.BlockSpec(memory_space=pltpu.HBM)] * 3,
        out_specs=(vmem,) * 7,
        scratch_shapes=[
            v(2, K, 48, C), v(K, 48, C), v(3, R, C), v(2, 4, 48, C), v(5, 4, R, C),
            v(2, 4, R, C), v(2, 4, 48, C), v(2, 2, R, C), v(2, 2, R, C), v(2, 4, R, C), v(2, 4, R, C), v(2, R, C), v(2, R, C),
            v(2, 4, 48, C), pltpu.VMEM((2, 4, R, 3 * C), BF16), pltpu.VMEM((5 * C, C), BF16),
            v(4, 112, C), v(2, R, C), v(2, 96, C), v(3, 112, C), v(2, R, C), v(2, 96, C),
            v(R, C), v(2, 8, C), v(2, 4, K, C), v(2, K, C),
            *surface, v(2, R, C), v(48, C),
            pltpu.SemaphoreType.DMA((9,)),
            pltpu.SemaphoreType.DMA((N_COPIES,)),
            pltpu.SemaphoreType.DMA((N_COPIES,)),
        ],
        compiler_params=pltpu.CompilerParams(
            collective_id=0, has_side_effects=True, vmem_limit_bytes=24 * 2**20),
        name="tendencies_and_surface",
    )(*(pltpu.with_memory_space_constraint(x, pltpu.HBM) for x in (layers, kmt, baro)))


LB = 10


def kernel_b(q, s, kmt_ref, a2d, baro, col, rows, out_hbm, baro_hbm, out, out_sem):
    lane = lanes()
    sub = sublanes((8, C))
    kmt = kmt_ref[...]
    au, av = a2d[0], a2d[1]
    kd = DT * KAPPA

    copies = [pltpu.make_async_copy(baro, baro_hbm, out_sem.at[K // LB])]
    copies[0].start()

    def tiles(x):
        return [x[8 * i:8 * i + 8] for i in range(4)]

    def from_north(x, halo):
        r = [pltpu.roll(t, 7, axis=0) for t in tiles(x)] + [jnp.broadcast_to(halo, (8, C))]
        return jnp.concatenate([jnp.where(sub == 7, r[i + 1], r[i]) for i in range(4)], axis=0)

    def from_south(x, halo):
        r = [jnp.broadcast_to(halo, (8, C))] + [pltpu.roll(t, 1, axis=0) for t in tiles(x)]
        return jnp.concatenate([jnp.where(sub == 0, r[i], r[i + 1]) for i in range(4)], axis=0)

    def level(k):
        c = k // CH
        j = k - c * CH
        tile = k // (2 * CH)
        back = 127 - 4 * j - 2 * (c - 2 * tile)
        m = k < kmt
        h = s[0, k]
        un = jnp.where(m, q[0, k] + au, 0.0)
        vn = jnp.where(m, q[1, k] + av, 0.0)
        out[0, k] = un
        out[1, k] = vn
        h5 = (0.5 * DT) * h
        fu, fv = h5 * un, h5 * vn

        def halo(n):
            return roll(col[n, tile], back)

        def row_n(n):
            return rows[4 + n, k:k + 1, :]

        def row_s(n):
            return rows[n, k:k + 1, :]

        hal = halo(0)
        e = jnp.where(lane == 127, hal, roll(fu, -1))
        w = jnp.where(lane == 0, hal, roll(fu, 1))
        hn = h - ((e - w) + (from_north(fv, row_n(0)) - from_south(fv, row_s(0))))
        out[2, k] = jnp.where(m, hn, 0.0)
        ke, kw, kn, ks = kd - fu, kd + fu, kd - fv, kd + fv
        mid = h - 4.0 * kd
        for n in range(1, 4):
            x = jnp.where(m, s[n, k], 0.0)
            hal = halo(n)
            e = jnp.where(lane == 127, hal, roll(x * ke, -1))
            w = jnp.where(lane == 0, hal, roll(x * kw, 1))
            r = from_north(x * kn, row_n(n)) + from_south(x * ks, row_s(n))
            out[2 + n, k] = jnp.where(m, (e + w) + (r + x * mid), 0.0)

    def put(i):
        at = slice(i * LB, (i + 1) * LB)
        return pltpu.make_async_copy(out.at[:, at], out_hbm.at[:, at], out_sem.at[i])

    for i in range(K // LB):
        for k in range(i * LB, (i + 1) * LB):
            level(k)
        put(i).start()
    for i in range(K // LB):
        put(i).wait()
    copies[0].wait()


def call_b(*operands):
    hbm = pl.BlockSpec(memory_space=pltpu.HBM)
    return pl.pallas_call(
        kernel_b,
        out_shape=(
            jax.ShapeDtypeStruct((6, K, R, C), F32),
            jax.ShapeDtypeStruct((3, R, C), F32),
        ),
        in_specs=[pl.BlockSpec(memory_space=pltpu.VMEM)] * len(operands),
        out_specs=(hbm, hbm),
        scratch_shapes=[
            pltpu.VMEM((6, K, R, C), F32),
            pltpu.SemaphoreType.DMA((K // LB + 1,)),
        ],
        compiler_params=pltpu.CompilerParams(vmem_limit_bytes=24 * 2**20),
        name="transport",
    )(*operands)


def per_device(layers, kmt, barotropic):
    return call_b(*call_a(layers, kmt, barotropic))


def solution(mesh):
    return jax.shard_map(
        per_device,
        mesh=mesh,
        in_specs=(P(None, None, "lat", "lon"), P("lat", "lon"), P(None, "lat", "lon")),
        out_specs=(P(None, None, "lat", "lon"), P(None, "lat", "lon")),
        check_vma=False,
    )
```

```python
import jax
import jax.numpy as jnp
from jax import lax
from jax.experimental import pallas as pl
from jax.experimental.pallas import tpu as pltpu
from jax.sharding import PartitionSpec as P

K = 100
NSUB = 16
R = 32
C = 128
CH = 25
UNROLL = 5
NY = 256

DT = 0.1
TAU = 0.6
NU = 0.01
KAPPA = 0.1
GRAV = 0.1
THERMAL = 1.0
HALINE = 0.8
ROT = 0.5

PSCALE = 1.0 / (4.0 * NU)

F32 = jnp.float32
BF16 = jnp.bfloat16
MESH = pl.DeviceIdType.MESH


def lanes(shape=(1, C)):
    return lax.broadcasted_iota(jnp.int32, shape, 1)


def sublanes(shape):
    return lax.broadcasted_iota(jnp.int32, shape, 0)


def split(x, parts):
    out = []
    for _ in range(parts):
        out.append(x.astype(BF16))
        x = x - out[-1].astype(F32)
    return jnp.concatenate(out, axis=1)


def roll(x, s):
    if isinstance(s, int):
        s %= C
        if s == 0:
            return x
    return pltpu.roll(x, s, axis=1)


def kernel_a(
    layers, kmt_hbm, baro_hbm,
    q, s, kmt_ref, a2d_out, baro_out, col_out, row_out,
    uv, p, baro_ref, cuv, cs,
    m_uv, r_uv, m_p, r_p, m_s, r_s, m_q, r_q,
    d4, corr, shift,
    b1, m1, r1, b2, m2, r2, a0v, r_a0v, r_rows, r_qrows,
    eta, ua, vv, dvv, da, dv, c2, c2a, cfa, cfv, sa, sv,
    load_sem, send_sem, recv_sem,
):
    lon = lax.axis_index("lon")
    lat = lax.axis_index("lat")
    nlon = lax.axis_size("lon")
    nlat = lax.axis_size("lat")
    east = lax.rem(lon + 1, nlon)
    west = lax.rem(lon + nlon - 1, nlon)
    north = lax.rem(lat + 1, nlat)
    south = lax.rem(lat + nlat - 1, nlat)
    x_of = {-1: west, 0: lon, 1: east}
    y_of = {-1: south, 0: lat, 1: north}

    loads = {}
    n_load = 0
    for name, src, dst in (("kmt", kmt_hbm, kmt_ref), ("baro", baro_hbm, baro_ref)):
        cp = pltpu.make_async_copy(src, dst, load_sem.at[n_load])
        cp.start()
        loads[name] = cp
        n_load += 1
    half = [slice(0, K // 2), slice(K // 2, K)]
    for i in range(2):
        cp = pltpu.make_async_copy(layers.at[0:2, half[i]], uv.at[0:2, half[i], 8:40, :], load_sem.at[n_load])
        cp.start()
        loads["uv", i] = cp
        n_load += 1
        for c in (2 * i, 2 * i + 1):
            cp = pltpu.make_async_copy(
                layers.at[2:5, c * CH:(c + 1) * CH], s.at[0:3, c * CH:(c + 1) * CH], load_sem.at[n_load])
            cp.start()
            loads["s", c] = cp
            n_load += 1
    cp = pltpu.make_async_copy(layers.at[5], s.at[3], load_sem.at[n_load])
    cp.start()
    loads["age"] = cp

    barrier = pltpu.get_barrier_semaphore()
    around = [(dx, dy) for dx in (-1, 0, 1) for dy in (-1, 0, 1) if (dx, dy) != (0, 0)]
    for dx, dy in around:
        pl.semaphore_signal(barrier, inc=1, device_id=(x_of[dx], y_of[dy]), device_id_type=MESH)

    copies = {}

    def send(name, src, dst, dx, dy):
        at = len(copies)
        cp = pltpu.make_async_remote_copy(
            src_ref=src, dst_ref=dst, send_sem=send_sem.at[at], recv_sem=recv_sem.at[at],
            device_id=(x_of[dx], y_of[dy]), device_id_type=MESH)
        cp.start()
        copies[name] = cp

    lane = lanes()
    quad = lane >> 2
    in_quad = lane & 3
    loads["kmt"].wait()
    loads["baro"].wait()
    kmt = kmt_ref[...]
    cmask = (kmt > 0).astype(F32)

    b1[1, 40:72, :] = baro_ref[1] * cmask
    b1[2, 40:72, :] = baro_ref[2] * cmask
    b1[3, 40:72, :] = kmt.astype(F32)

    def pack(fields):
        def body(j, accs):
            sel = quad == j
            xs = []
            for load, masked, _, _, c in fields:
                k = c * CH + j
                x = load(k)
                xs.append(jnp.where(k < kmt, x, 0.0) if masked else x)
            out = tuple(jnp.where(sel, roll(x, 4 * j + 2), acc) for x, acc in zip(xs, accs))
            for x, (_, _, store, _, c) in zip(xs, fields):
                if store is not None:
                    uv[store, c * CH + j, 8:40, :] = x
            return out

        accs = lax.fori_loop(0, CH, body, (jnp.zeros((R, C), F32),) * len(fields), unroll=UNROLL)
        for (_, _, _, put, c), acc in zip(fields, accs):
            put(c, acc)

    def put_cuv(f):
        def put(c, x):
            cuv[f, c, 8:40, :] = x
        return put

    def put_cs(f):
        def put(c, x):
            cs[f, c] = x
        return put

    def velocities(i):
        return [(lambda k, f=f: uv[f, k, 8:40, :], True, f, put_cuv(f), c) for f in range(2) for c in (2 * i, 2 * i + 1)]

    def pressures(i):
        return [(lambda k: p[k, 8:40, :], False, None, put_cs(0), c) for c in (2 * i, 2 * i + 1)]

    def scalars(f):
        return [(lambda k: s[f, k], True, None, put_cs(1 + f), c) for c in range(4)]

    def compact(field, lane_from, chunks=(0, 1, 2, 3)):
        out = roll(cs[field, chunks[0]], chunks[0] - lane_from)
        for c in chunks[1:]:
            out = jnp.where(in_quad == c, roll(cs[field, c], c - lane_from), out)
        return out

    def send_velocities(i):
        both = slice(2 * i, 2 * i + 2)
        for c in (2 * i, 2 * i + 1):
            cu, cv = cuv[0, c, 8:40, :], cuv[1, c, 8:40, :]
            m_uv[0, c] = jnp.where(in_quad < 2, cu, roll(cv, 2))
            m_uv[1, c] = jnp.where(in_quad < 2, roll(cu, -2), cv)
        for d, dx in ((0, 1), (1, -1)):
            send(("uv", dx, 1, i), m_uv.at[d, both, 31:32, :], r_uv.at[d, both, 7:8, :], dx, 1)
            send(("uv", dx, -1, i), m_uv.at[d, both, 0:1, :], r_uv.at[d, both, 40:41, :], dx, -1)
            send(("uv", dx, 0, i), m_uv.at[d, both], r_uv.at[d, both, 8:40, :], dx, 0)
        send(("cuv_n", i), cuv.at[:, both, 39:40, :], cuv.at[:, both, 7:8, :], 0, 1)
        send(("cuv_s", i), cuv.at[:, both, 8:9, :], cuv.at[:, both, 40:41, :], 0, -1)

    def send_pressures(i):
        m_p[i, 0] = compact(0, 1, (2 * i, 2 * i + 1))
        m_p[i, 1] = compact(0, 2, (2 * i, 2 * i + 1))
        send(("p_e", i), m_p.at[i, 0], r_p.at[i, 0], 1, 0)
        send(("p_w", i), m_p.at[i, 1], r_p.at[i, 1], -1, 0)
        send(("p_n", i), p.at[half[i], 39, :], p.at[half[i], 7, :], 0, 1)
        send(("p_s", i), p.at[half[i], 8, :], p.at[half[i], 40, :], 0, -1)

    loads["uv", 0].wait()
    pack(velocities(0))

    pl.semaphore_wait(barrier, 8)
    for i in range(2):
        send(("uv_n", i), layers.at[0:2, half[i], 30:32, :], uv.at[:, half[i], 6:8, :], 0, 1)
        send(("uv_s", i), layers.at[0:2, half[i], 0:2, :], uv.at[:, half[i], 40:42, :], 0, -1)
        if i == 0:
            send("b1_n", b1.at[1:4, 40:72, :], b1.at[1:4, 8:40, :], 0, 1)
            send("b1_s", b1.at[1:4, 40:72, :], b1.at[1:4, 72:104, :], 0, -1)
    send_velocities(0)

    zero = jnp.zeros((R, C), F32)
    csum, total = zero, zero
    for c in range(4):
        loads["s", c].wait()

        def body(j, carry, c=c):
            csum, total = carry
            k = c * CH + j
            m = k < kmt
            h = jnp.where(m, s[0, k], 0.0)
            w = ((PSCALE * GRAV * HALINE) * s[2, k] - (PSCALE * GRAV * THERMAL) * s[1, k]) * h
            pk = csum + 0.5 * w
            p[k, 8:40, :] = pk
            return csum + w, total + h

        csum, total = lax.fori_loop(0, CH, body, (csum, total), unroll=UNROLL)
        if c == 1:
            loads["uv", 1].wait()
            pack(pressures(0) + velocities(1))
            send_pressures(0)
            send_velocities(1)

    b1[0, 40:72, :] = total * (1.0 / K)

    def side(fields, eastward):
        out = None
        for n, x in enumerate(fields):
            moved = roll(x, 32 * n + 32) if eastward else roll(x, 32 * n)
            out = moved if out is None else jnp.where(lane < 32 * n, out, moved)
        return out

    def unside(n, d):
        return (roll(d[0], 96 - 32 * n), roll(d[1], -32 * n))

    mine = [b1[n, 40:72, :] for n in range(3)]
    m1[0] = side(mine, True)
    m1[1] = side(mine, False)

    def send_sides(tag, m, r):
        for d, dx in ((0, 1), (1, -1)):
            send((tag, dx, 1), m.at[d], r.at[d, 0:32, :], dx, 1)
            send((tag, dx, -1), m.at[d], r.at[d, 64:96, :], dx, -1)
            send((tag, dx, 0), m.at[d], r.at[d, 32:64, :], dx, 0)

    send("d_n", b1.at[0, 40:72, :], b1.at[0, 8:40, :], 0, 1)
    send("d_s", b1.at[0, 40:72, :], b1.at[0, 72:104, :], 0, -1)
    send_sides("b1", m1, r1)

    def send_scalars(which):
        for f in which:
            m_s[0, f] = compact(1 + f, 1)
            m_s[1, f] = compact(1 + f, 2)

    pack(pressures(1) + scalars(0))
    send_pressures(1)
    pack(scalars(1))
    loads["age"].wait()
    send("s_n", s.at[:, :, 31, :], r_rows.at[0], 0, 1)
    send("s_s", s.at[:, :, 0, :], r_rows.at[1], 0, -1)

    def tiles_of(n, centre, r, at):
        lo, hi = at
        t0 = centre[n, 8 + lo:8 + hi, :]
        from_west, from_east = unside(n, (r[0, lo:hi, :], r[1, lo:hi, :]))
        t1 = jnp.where(lane < 32, from_east, jnp.where(lane >= 96, from_west, 0.0))
        return t0, t1

    def shift_west(t0, t1):
        a, b = roll(t0, 1), roll(t1, 1)
        return jnp.where(lane < 1, b, a), jnp.where(lane < 1, a, b)

    def next_height(lo, both):
        n = 2 if both else 1
        at = pl.ds(lo, 8)
        x = [da[t, at, :] * ua[t, at, :] for t in range(2)]
        r = [roll(x[t], -2) for t in range(2)]
        out = []
        for t in range(n):
            diff = jnp.where(lane < 126, r[t], r[1 - t]) - x[t]
            diff = diff + (dvv[t, pl.ds(lo + 1, 8), :] - dvv[t, pl.ds(lo - 1, 8), :])
            out.append(c2[t, at, :] * diff)
        return out

    def prepare_surface():
        for name in ("d_n", "d_s"):
            copies[name].wait_recv()
        for dx in (1, -1):
            for dy in (0, 1, -1):
                copies["b1", dx, dy].wait_recv()
        for ref in (eta, dvv):
            for t in range(2):
                ref[t, 0:8, :] = jnp.zeros((8, C), F32)
                ref[t, 104:112, :] = jnp.zeros((8, C), F32)
        for blk in range(3):
            at = (32 * blk, 32 * blk + 32)
            here = slice(8 + 32 * blk, 40 + 32 * blk)
            dd = tiles_of(0, b1, r1, at)
            uu = tiles_of(1, b1, r1, at)
            ww = tiles_of(2, b1, r1, at)
            dda = shift_west(*dd)
            uua = shift_west(*uu)
            for t in range(2):
                da[t, here, :] = dda[t]
                ua[t, here, :] = uua[t]
                dv[t, here, :] = dd[t]
                vv[t, here, :] = ww[t]
                dvv[t, here, :] = dd[t] * ww[t]
                c2[t, here, :] = jnp.where(dd[t] > 0.0, 0.5 * TAU, 0.0)
                c2a[t, here, :] = jnp.where(dda[t] > 0.0, 0.5 * TAU, 0.0)

        for i in range(4):
            drop = next_height(40 + 8 * i, False)[0]
            b2[2, 40 + 8 * i:48 + 8 * i, :] = (
                baro_ref[0, 8 * i:8 * i + 8, :] * cmask[8 * i:8 * i + 8] - drop)

    def correct(i):
        for name in ("cuv_n", "cuv_s", "p_e", "p_w", "uv_n", "uv_s", "p_n", "p_s"):
            copies[name, i].wait_recv()
        for dx in (1, -1):
            for dy in (0, 1, -1):
                copies["uv", dx, dy, i].wait_recv()
        p_w, p_e = r_p[i, 0], r_p[i, 1]
        for c in (2 * i, 2 * i + 1):
            w, e = r_uv[0, c], r_uv[1, c]
            d4[0, c] = jnp.where(in_quad < 2, w, roll(e, 2)) - cuv[0, c]
            d4[1, c] = jnp.where(in_quad < 2, roll(w, -2), e) - cuv[1, c]
        for c in (2 * i, 2 * i + 1):
            for f in range(2):
                x = d4[f, c, 8:40, :]
                g = 2.0 * (d4[f, c, 9:41, :] + d4[f, c, 7:39, :]) - 8.0 * x
                out = jnp.where(in_quad < 2, roll(x, -2), roll(x, 2))
                out = out + jnp.where(in_quad == 1, roll(g, -1), jnp.where(in_quad == 2, roll(g, 1), 0.0))
                out = 0.5 * out
                if f == 0:
                    own = cs[0, c]
                    at_127 = roll(p_e, 1 - c) - roll(own, -1)
                    at_0 = roll(own, 1) - roll(p_w, 2 - c)
                    out = out + jnp.where(in_quad == 1, at_127, jnp.where(in_quad == 2, at_0, 0.0))
                corr[f, c] = split(out, 3)

    for name in ("b1_n", "b1_s"):
        copies[name].wait_recv()

    row = sublanes((R, C)) + lat * R
    cor = DT * ROT * (2.0 * (row.astype(F32) + 0.5) / NY - 1.0)

    rim = {at: b1[3, at + 32:at + 40, :] for at in (6, 7, 33, 34)}

    def shifted(f, k, by, seen):
        lo = 8 + by
        x = uv[f, k, lo:lo + R, :]
        at = lo if by < 0 else lo + 24
        if by < 0:
            return jnp.concatenate([jnp.where(seen[at], x[0:8], 0.0), x[8:]], axis=0)
        return jnp.concatenate([x[:24], jnp.where(seen[at], x[24:], 0.0)], axis=0)

    def stencil(f, k, seen):
        x = uv[f, k, 8:40, :]
        one = shifted(f, k, 1, seen) + shifted(f, k, -1, seen)
        two = shifted(f, k, 2, seen) + shifted(f, k, -2, seen)
        return x, one - 4.0 * x, 0.5 * two + (10.0 * x - 4.0 * one)

    i = lax.broadcasted_iota(jnp.int32, (5 * C, C), 0)
    to = lax.broadcasted_iota(jnp.int32, (5 * C, C), 1)
    apart = (to - i) & (C - 1)
    far = jnp.where((apart == 2) | (apart == C - 2), 0.5, 0.0)
    edge = jnp.where(to == ((126 + (i & 3)) & (C - 1)), 1.0, 0.0)
    shift[...] = jnp.where(i < 2 * C, far, edge).astype(BF16)
    quad3 = lax.broadcasted_iota(jnp.int32, (1, 3 * C), 1) % C >> 2

    def level(k, extra, sums):
        sgu, sgv, squ, sqv = sums
        m = k < kmt
        kf = k.astype(F32)
        seen = {at: kf < x for at, x in rim.items()}
        u0, unear, gu = stencil(0, k, seen)
        v0, vnear, gv = stencil(1, k, seen)
        pk = p[k, 8:40, :]
        ue = roll(unear + pk, -1)
        uw = roll(unear - pk, 1)
        ve, vw = roll(vnear, -1), roll(vnear, 1)
        gv = gv + (p[k, 9:41, :] - p[k, 7:39, :])
        gu = (gu + extra[0]) + (ue + uw)
        gv = (gv + extra[1]) + (ve + vw)
        gu = jnp.where(m, cor * v0 - (2.0 * DT * NU) * gu, 0.0)
        gv = jnp.where(m, -cor * u0 - (2.0 * DT * NU) * gv, 0.0)
        qu = u0 + gu
        qv = v0 + gv
        q[0, k] = qu
        q[1, k] = qv
        h = s[0, k]
        return sgu + gu * h, sgv + gv * h, squ + qu * h, sqv + qv * h

    sums = (zero,) * 4
    for i in range(2):
        correct(i)

        def body(n, sums):
            c = n // 5
            j0 = 5 * (n - 5 * c)
            left = [], []
            for l in range(5):
                on = (quad3 == j0 + l).astype(F32).astype(BF16)
                for f in range(2):
                    deep = (5 - f) * C - 2 * C
                    left[f].append(jnp.concatenate([split(uv[f, 5 * n + l, 8:40, :], 2), (corr[f, c] * on)[:, :deep]], axis=1))
            moved = [
                jnp.dot(jnp.concatenate(left[f], axis=0), shift[:(5 - f) * C, :], preferred_element_type=F32)
                for f in range(2)
            ]
            for l in range(5):
                extra = [moved[f][R * l:R * (l + 1)] for f in range(2)]
                sums = level(5 * n + l, extra, sums)
            return sums

        sums = lax.fori_loop(10 * i, 10 * i + 10, body, sums, unroll=2)
        if i == 0:
            prepare_surface()
    sgu, sgv, squ, sqv = sums

    bound = jnp.maximum(total, 1.0)
    fu, fv = (1.0 / DT) * sgu / bound, (1.0 / DT) * sgv / bound
    a0u = -DT * fu - (squ - DT * fu * total) / bound
    a0v[...] = -DT * fv - (sqv - DT * fv * total) / bound
    b2[0, 40:72, :] = fu
    b2[1, 40:72, :] = fv
    mine = [fu, fv, b2[2, 40:72, :], a0u]
    m2[0] = side(mine, True)
    m2[1] = side(mine, False)
    send_sides("b2", m2, r2)
    send("b2_n", b2.at[:, 40:72, :], b2.at[:, 8:40, :], 0, 1)
    send("b2_s", b2.at[:, 40:72, :], b2.at[:, 72:104, :], 0, -1)
    send("a_n", a0v.at[24:32, :], r_a0v.at[0], 0, 1)
    send("a_s", a0v.at[0:8, :], r_a0v.at[1], 0, -1)
    send("q_n", q.at[1, :, 31, :], r_qrows.at[0], 0, 1)
    send("q_s", q.at[1, :, 0, :], r_qrows.at[1], 0, -1)
    pack([(lambda k: q[0, k], False, None, put_cs(0), c) for c in range(4)] + scalars(2))
    m_q[0] = compact(0, 1)
    m_q[1] = compact(0, 2)
    send("q_e", m_q.at[0], r_q.at[0], 1, 0)
    send("q_w", m_q.at[1], r_q.at[1], -1, 0)
    pack(scalars(3))
    send_scalars(range(4))
    send("s_e", m_s.at[0], r_s.at[0], 1, 0)
    send("s_w", m_s.at[1], r_s.at[1], -1, 0)

    for name in ("b2_n", "b2_s"):
        copies[name].wait_recv()
    for dx in (1, -1):
        for dy in (0, 1, -1):
            copies["b2", dx, dy].wait_recv()
    for blk in range(3):
        at = (32 * blk, 32 * blk + 32)
        here = slice(8 + 32 * blk, 40 + 32 * blk)
        ffu = shift_west(*tiles_of(0, b2, r2, at))
        ffv = tiles_of(1, b2, r2, at)
        ee = tiles_of(2, b2, r2, at)
        for t in range(2):
            eta[t, here, :] = ee[t]
            cfa[t, here, :] = 2.0 * c2a[t, here, :] * ffu[t]
            cfv[t, here, :] = 2.0 * c2[t, here, :] * ffv[t]

    sa[...] = jnp.zeros((2, R, C), F32)
    sv[...] = jnp.zeros((48, C), F32)

    def flows(first, count):
        for i in range(count):
            lo = 8 + 8 * (first + i)
            at = slice(lo, lo + 8)
            e = [eta[t, at, :] for t in range(2)]
            r = [roll(e[t], 2) for t in range(2)]
            for t in range(2):
                diff = e[t] - jnp.where(lane < 2, r[1 - t], r[t])
                new_u = ua[t, at, :] + (cfa[t, at, :] - c2a[t, at, :] * diff)
                ua[t, at, :] = new_u
                diff = eta[t, lo + 1:lo + 9, :] - eta[t, lo - 1:lo + 7, :]
                new_v = vv[t, at, :] + (cfv[t, at, :] - c2[t, at, :] * diff)
                vv[t, at, :] = new_v
                dvv[t, at, :] = dv[t, at, :] * new_v
                if 40 <= lo < 72:
                    sa[t, lo - 40:lo - 32, :] += new_u
                if t == 0 and 32 <= lo < 80:
                    sv[lo - 32:lo - 24, :] += new_v

    def heights(first, count):
        for i in range(count):
            lo = 8 + 8 * (first + i)
            drop = next_height(lo, True)
            for t in range(2):
                eta[t, lo:lo + 8, :] = eta[t, lo:lo + 8, :] - drop[t]

    flows(0, 12)
    for group in range(4):
        first, count = group, 12 - 2 * group

        def body(n, carry, first=first, count=count):
            heights(first, count)
            flows(first, count)
            return carry

        lax.fori_loop(0, 3 if group == 0 else 4, body, 0)

    sa0, sa1 = sa[0], sa[1]
    su = jnp.where(lane < 127, roll(sa0, -1), roll(sa1, -1))
    a2d_out[0] = a0u + su * (1.0 / NSUB)
    a2d_out[1] = a0v[...] + sv[8:40, :] * (1.0 / NSUB)
    baro_out[0] = eta[0, 40:72, :]
    baro_out[1] = jnp.where(lane < 127, roll(ua[0, 40:72, :], -1), roll(ua[1, 40:72, :], -1))
    baro_out[2] = vv[0, 40:72, :]

    for name in ("s_e", "s_w", "q_e", "q_w"):
        copies[name].wait_recv()
    a_w = r2[0, 32:64, 127:128] + sa0[:, 0:1] * (1.0 / NSUB)
    a_e = r2[1, 32:64, 96:97] + sa1[:, 1:2] * (1.0 / NSUB)
    halves = []
    for d, a, sign in ((0, a_w, 1.0), (1, a_e, -1.0)):
        flux = (0.5 * DT) * r_s[d, 0] * (r_q[d] + a)
        vals = [flux]
        for n in range(1, 4):
            vals.append(r_s[d, n] * ((DT * KAPPA) + sign * flux))
        halves.append(vals)
    for n in range(4):
        w, e = halves[0][n], halves[1][n]
        col_out[n, 0] = jnp.where(
            in_quad == 0, e, jnp.where(in_quad == 1, roll(w, 1), jnp.where(in_quad == 2, roll(e, 1), roll(w, 2))))
        col_out[n, 1] = jnp.where(
            in_quad == 0, roll(e, -2), jnp.where(in_quad == 1, roll(w, -1), jnp.where(in_quad == 2, roll(e, -1), w)))

    for name in ("s_n", "s_s", "q_n", "q_s", "a_n", "a_s"):
        copies[name].wait_recv()
    level = sublanes((K, C)).astype(F32)
    for d, kmt_row, a_row, sign in (
        (0, b1[3, 39:40, :], r_a0v[0, 7:8, :] + sv[7:8, :] * (1.0 / NSUB), 1.0),
        (1, b1[3, 72:73, :], r_a0v[1, 0:1, :] + sv[40:41, :] * (1.0 / NSUB), -1.0),
    ):
        m = level < kmt_row
        flux = jnp.where(m, (0.5 * DT) * r_rows[d, 0] * (r_qrows[d] + a_row), 0.0)
        row_out[4 * d] = flux
        for n in range(1, 4):
            row_out[4 * d + n] = jnp.where(m, r_rows[d, n], 0.0) * ((DT * KAPPA) + sign * flux)

    for cp in copies.values():
        cp.wait_send()


N_COPIES = 2 * (2 + 8 + 4) + 10 + 4 + 14


def call_a(layers, kmt, baro):
    v = lambda *shape: pltpu.VMEM(shape, F32)
    surface = [v(2, 112, C) for _ in range(10)]
    vmem = pl.BlockSpec(memory_space=pltpu.VMEM)
    shape = lambda *dims: jax.ShapeDtypeStruct(dims, F32)
    return pl.pallas_call(
        kernel_a,
        out_shape=(
            shape(2, K, R, C), shape(4, K, R, C), jax.ShapeDtypeStruct((R, C), jnp.int32),
            shape(2, R, C), shape(3, R, C), shape(4, 2, R, C), shape(8, K, C),
        ),
        in_specs=[pl.BlockSpec(memory_space=pltpu.HBM)] * 3,
        out_specs=(vmem,) * 7,
        scratch_shapes=[
            v(2, K, 48, C), v(K, 48, C), v(3, R, C), v(2, 4, 48, C), v(5, 4, R, C),
            v(2, 4, R, C), v(2, 4, 48, C), v(2, 2, R, C), v(2, 2, R, C), v(2, 4, R, C), v(2, 4, R, C), v(2, R, C), v(2, R, C),
            v(2, 4, 48, C), pltpu.VMEM((2, 4, R, 3 * C), BF16), pltpu.VMEM((5 * C, C), BF16),
            v(4, 112, C), v(2, R, C), v(2, 96, C), v(3, 112, C), v(2, R, C), v(2, 96, C),
            v(R, C), v(2, 8, C), v(2, 4, K, C), v(2, K, C),
            *surface, v(2, R, C), v(48, C),
            pltpu.SemaphoreType.DMA((9,)),
            pltpu.SemaphoreType.DMA((N_COPIES,)),
            pltpu.SemaphoreType.DMA((N_COPIES,)),
        ],
        compiler_params=pltpu.CompilerParams(
            collective_id=0, has_side_effects=True, vmem_limit_bytes=24 * 2**20),
        name="tendencies_and_surface",
    )(*(pltpu.with_memory_space_constraint(x, pltpu.HBM) for x in (layers, kmt, baro)))


LB = 10


def kernel_b(q, s, kmt_ref, a2d, baro, col, rows, out_hbm, baro_hbm, out, out_sem):
    lane = lanes()
    sub = sublanes((8, C))
    kmt = kmt_ref[...]
    au, av = a2d[0], a2d[1]
    kd = DT * KAPPA

    copies = [pltpu.make_async_copy(baro, baro_hbm, out_sem.at[K // LB])]
    copies[0].start()

    def tiles(x):
        return [x[8 * i:8 * i + 8] for i in range(4)]

    def from_north(x, halo):
        r = [pltpu.roll(t, 7, axis=0) for t in tiles(x)] + [jnp.broadcast_to(halo, (8, C))]
        return jnp.concatenate([jnp.where(sub == 7, r[i + 1], r[i]) for i in range(4)], axis=0)

    def from_south(x, halo):
        r = [jnp.broadcast_to(halo, (8, C))] + [pltpu.roll(t, 1, axis=0) for t in tiles(x)]
        return jnp.concatenate([jnp.where(sub == 0, r[i], r[i + 1]) for i in range(4)], axis=0)

    def level(k):
        c = k // CH
        j = k - c * CH
        tile = k // (2 * CH)
        back = 127 - 4 * j - 2 * (c - 2 * tile)
        m = k < kmt
        h = s[0, k]
        un = jnp.where(m, q[0, k] + au, 0.0)
        vn = jnp.where(m, q[1, k] + av, 0.0)
        out[0, k] = un
        out[1, k] = vn
        h5 = (0.5 * DT) * h
        fu, fv = h5 * un, h5 * vn

        def halo(n):
            return roll(col[n, tile], back)

        def row_n(n):
            return rows[4 + n, k:k + 1, :]

        def row_s(n):
            return rows[n, k:k + 1, :]

        hal = halo(0)
        e = jnp.where(lane == 127, hal, roll(fu, -1))
        w = jnp.where(lane == 0, hal, roll(fu, 1))
        hn = h - ((e - w) + (from_north(fv, row_n(0)) - from_south(fv, row_s(0))))
        out[2, k] = jnp.where(m, hn, 0.0)
        ke, kw, kn, ks = kd - fu, kd + fu, kd - fv, kd + fv
        mid = h - 4.0 * kd
        for n in range(1, 4):
            x = jnp.where(m, s[n, k], 0.0)
            hal = halo(n)
            e = jnp.where(lane == 127, hal, roll(x * ke, -1))
            w = jnp.where(lane == 0, hal, roll(x * kw, 1))
            r = from_north(x * kn, row_n(n)) + from_south(x * ks, row_s(n))
            out[2 + n, k] = jnp.where(m, (e + w) + (r + x * mid), 0.0)

    def put(i):
        at = slice(i * LB, (i + 1) * LB)
        return pltpu.make_async_copy(out.at[:, at], out_hbm.at[:, at], out_sem.at[i])

    for i in range(K // LB):
        for k in range(i * LB, (i + 1) * LB):
            level(k)
        put(i).start()
    for i in range(K // LB):
        put(i).wait()
    copies[0].wait()


def call_b(*operands):
    hbm = pl.BlockSpec(memory_space=pltpu.HBM)
    return pl.pallas_call(
        kernel_b,
        out_shape=(
            jax.ShapeDtypeStruct((6, K, R, C), F32),
            jax.ShapeDtypeStruct((3, R, C), F32),
        ),
        in_specs=[pl.BlockSpec(memory_space=pltpu.VMEM)] * len(operands),
        out_specs=(hbm, hbm),
        scratch_shapes=[
            pltpu.VMEM((6, K, R, C), F32),
            pltpu.SemaphoreType.DMA((K // LB + 1,)),
        ],
        compiler_params=pltpu.CompilerParams(vmem_limit_bytes=24 * 2**20),
        name="transport",
    )(*operands)


def per_device(layers, kmt, barotropic):
    return call_b(*call_a(layers, kmt, barotropic))


def solution(mesh):
    return jax.shard_map(
        per_device,
        mesh=mesh,
        in_specs=(P(None, None, "lat", "lon"), P("lat", "lon"), P(None, "lat", "lon")),
        out_specs=(P(None, None, "lat", "lon"), P(None, "lat", "lon")),
        check_vma=False,
    )
```
